128 devices in a mesh: sky: 64 (over x, y, z), band: 2 (over core).
Axes of the slice: x: 4, y: 4, z: 4, core: 2. Of those that a mesh axis runs over, the one named last changes fastest.
Arguments:
- stamps: bfloat16 [16384, 6, 2304], P('sky', 'band'), may hold values from 0 to 2
- stamp_gain: bfloat16 [16384], P('sky'), may hold values from 0.5 to 2
- stamp_invvar: bfloat16 [16384], P('sky'), may hold values from 1 to 10
- stamp_dest: int32 [16384, 1], P('sky'), may hold values from 0 to 63; in each aligned block of 256 rows (0 to 255, 256 to 511, ...) at most 8 rows name the same one
- stamp_obj: int32 [16384], P('sky'), may hold values from 0 to 63
- phi_tpl: bfloat16 [6, 16, 2304], P('band'), may hold values from 0 to 0.041503906
- psi_tpl: bfloat16 [6, 16, 2304], P('band'), may hold values from 0 to 0.041503906
- theta_init: float32 [16, 4096], P(None, 'sky'), may hold values from -3 to 3
- nb_id: int32 [4096, 4], P('sky'), may hold values from 0 to 4095, as said below
- nb_weight: float32 [4096, 4], P('sky'), may hold values from 0.2 to 0.8
Outputs:
- theta_fit: float32 [16, 4096], P(None, 'sky')
The draws below stay inside these ranges and needn't reach their ends.
Inputs may be any that keep to these rules, and one draw needn't show every extreme that they name: `stamp_dest`: among the stamps of one index of sky no destination is named more than 8 times, a bound that some block reaches. `nb_id`: each neighbour is owned by the object's own index of sky or by the index just before or after it, cyclically.
All inputs are finite; a program needn't handle non-finite values.
Results may differ from the reference program's by a relative error of at most 0.0007.
Values may be sent and summed in bfloat16 or wider, within the bound.
A program may use at most 128 MiB of HBM per device.

```python
import math
import jax
import jax.numpy as jnp
import numpy as np
from jax import lax

BANDS = 6
K = 16
NEI = 4
ITERS = 3
STAMP_DEV = 256
OBJ_DEV = 64
PIX = 2304
CAP = 8
STAMPS = 16384
OBJECTS = 4096
N_SKY = 64


def draw_nb_id(key, part):
    first_key, second_key = jax.random.split(jax.random.fold_in(key, 7))
    home = jnp.arange(OBJECTS, dtype=jnp.int32)[:, None] // OBJ_DEV
    offset = jax.random.randint(first_key, (OBJECTS, NEI), -1, 2).astype(jnp.int32)
    local = jax.random.randint(second_key, (OBJECTS, NEI), 0, OBJ_DEV).astype(jnp.int32)
    return (jnp.mod(home + offset, N_SKY) * OBJ_DEV + local).astype(jnp.int32)


def touch_ends(result, own_key, smallest, largest):
    longest = result.shape.index(max(result.shape))
    spots = []
    for shift in (0, 1):
        where = [jax.random.randint(jax.random.fold_in(own_key, axis), (), 0, length) for axis, length in enumerate(result.shape)]
        where[longest] = (where[longest] + shift) % result.shape[longest]
        spots.append(tuple(where))
    return result.at[spots[0]].set(smallest).at[spots[1]].set(largest)


def block_scale(stream_key, shape, cuts, low, top_value):
    level = 1.0
    for dim, shards_of in cuts:
        steps = jax.random.uniform(jax.random.fold_in(jax.random.fold_in(stream_key, 6), dim), (shards_of,), jnp.float32, low / len(cuts), top_value / len(cuts))
        level = level * jnp.repeat(jnp.exp(steps), shape[dim] // shards_of).reshape((-1,) + (1,) * (len(shape) - 1 - dim))
    return level


def shared_out(key, own, number, rows, amount, top, bound, slope):
    order = jax.random.permutation(key, amount)
    packed, common = shares(amount, rows * top, bound, slope, True), shares(amount, rows * top, bound, slope, False)
    places = jnp.arange(amount)

    def named(lengths, rotation):
        used = int((lengths > 0).sum())
        fixed = max(1, used // 4)
        shifted = fixed + (places - fixed + rotation * (used - fixed)) % max(1, amount - fixed)
        return jnp.zeros((amount,), jnp.int32).at[order[jnp.where(places < fixed, places, shifted)]].set(jnp.asarray(lengths, jnp.int32))

    lengths = jnp.where(number % 4 == 0, named(packed, number // 4), named(common, number - number // 4 - 1))
    mixed = jax.random.permutation(jax.random.fold_in(own, 3), amount)
    donor, sink = mixed[0:amount // 2 * 2:2], mixed[1:amount // 2 * 2:2]
    margin = jnp.minimum(lengths[donor] - 1, bound - lengths[sink]) // 2
    margin = jnp.where((donor == order[0]) | (sink == order[0]) | (lengths[sink] == 0), 0, jnp.maximum(margin, 0))
    shifted = jax.random.randint(jax.random.fold_in(own, 4), (amount // 2,), 0, 1 << 20) % (margin + 1)
    lengths = lengths.at[donor].add(-shifted).at[sink].add(shifted)
    labels = jnp.searchsorted(jnp.cumsum(lengths), jnp.arange(rows * top), side="right").astype(jnp.int32)
    listing = labels.reshape(top, rows).T
    listing = listing[jax.random.permutation(jax.random.fold_in(own, 1), rows)]
    rotation = jax.random.randint(jax.random.fold_in(own, 2), (rows, 1), 0, top)
    return jnp.take_along_axis(listing, (jnp.arange(top)[None, :] + rotation) % top, axis=1)


def shares(count, total, most, lean, full):
    weights = [(1 << 20) // math.isqrt(rank ** lean) + 1 for rank in range(1, count + 1)]
    largest = most if full else min(most, max(-(-total // count), total * weights[0] // sum(weights)))
    least = 1 if total - largest >= count - 1 else 0
    given, surplus = [largest] + [least] * (count - 1), total - largest - least * (count - 1)
    while surplus > 0:
        candidates = [i for i in range(1, count) if given[i] < largest] or [i for i in range(1, count) if given[i] < most]
        mass, remaining = sum([weights[i] for i in candidates]), surplus
        for i in candidates:
            addition = min(most - given[i], max(1, remaining * weights[i] // mass), surplus)
            given[i] = given[i] + addition
            surplus = surplus - addition
    return np.array(given)


def normal_values(stream_key, shape, spread, limit, shards=(), kind=jnp.bfloat16):
    loudness = block_scale(stream_key, shape, shards, -0.22, 0.18) if shards else 1.0
    values = jax.random.normal(stream_key, shape, jnp.float32) * spread * loudness
    return jnp.minimum(jnp.maximum(values, -limit), limit).astype(kind)


def setup_inputs(seed: int = 0) -> dict:
    splits = jax.random.split(jax.random.key(seed), 11)
    stamps = jnp.clip(2.0 * jax.random.uniform(splits[0], (STAMPS, BANDS, PIX), jnp.float32) ** block_scale(splits[0], (STAMPS, BANDS, PIX), ((0, 64), (1, 2)), -0.2, 0.2), 0.0, 2.0).astype(jnp.bfloat16)
    stamp_gain = jnp.clip(jnp.exp(math.log(2.0) - 1.3862944 * jax.random.uniform(splits[1], (STAMPS,), jnp.float32) ** block_scale(splits[1], (STAMPS,), ((0, 64),), -0.2, 0.2)), 0.5, 2.0).astype(jnp.bfloat16)
    stamp_invvar = jnp.clip(jnp.exp(math.log(10.0) - 2.3025851 * jax.random.uniform(splits[2], (STAMPS,), jnp.float32) ** block_scale(splits[2], (STAMPS,), ((0, 64),), -0.2, 0.2)), 1.0, 10.0).astype(jnp.bfloat16)
    stamp_dest_keys = jax.random.split(jax.random.fold_in(splits[3], 1), STAMPS // STAMP_DEV)
    stamp_dest_turns = jax.random.permutation(jax.random.fold_in(splits[3], 3), STAMPS // STAMP_DEV)
    stamp_dest = jax.vmap(lambda own, number: shared_out(jax.random.fold_in(splits[3], 2), own, number, STAMP_DEV, N_SKY, 1, CAP, 2))(stamp_dest_keys, stamp_dest_turns).reshape((STAMPS, 1))
    stamp_obj = touch_ends(jax.random.randint(splits[4], (STAMPS,), 0, OBJ_DEV), jax.random.fold_in(splits[4], 1), 0, OBJ_DEV - 1).astype(jnp.int32)
    phi_tpl = jnp.clip(0.041503906 * jax.random.uniform(splits[5], (BANDS, K, PIX), jnp.float32) ** block_scale(splits[5], (BANDS, K, PIX), ((0, 2),), -0.2, 0.2), 0.0, 0.041503906).astype(jnp.bfloat16)
    psi_tpl = jnp.clip(0.041503906 * jax.random.uniform(splits[6], (BANDS, K, PIX), jnp.float32) ** block_scale(splits[6], (BANDS, K, PIX), ((0, 2),), -0.2, 0.2), 0.0, 0.041503906).astype(jnp.bfloat16)
    theta_init = normal_values(splits[7], (K, OBJECTS), 0.5, 3.0, ((1, 64),), jnp.float32)
    nb_id = draw_nb_id(jax.random.fold_in(splits[10], 71), 0)
    nb_weight = jnp.clip(0.2 + 0.6 * jax.random.uniform(splits[9], (OBJECTS, NEI), jnp.float32) ** block_scale(splits[9], (OBJECTS, NEI), ((0, 64),), -0.2, 0.2), 0.2, 0.8)
    return dict(stamps=stamps, stamp_gain=stamp_gain, stamp_invvar=stamp_invvar, stamp_dest=stamp_dest, stamp_obj=stamp_obj, phi_tpl=phi_tpl, psi_tpl=psi_tpl, theta_init=theta_init, nb_id=nb_id, nb_weight=nb_weight)


ROBUST = 9.0
DAMPING = 0.1
PRIOR = 1.0
STEP_LIMIT = 0.5


def batch_solve(matrix, target):
    size_k = matrix.shape[0]
    for pivot_row in range(size_k):
        pivot_value = matrix[pivot_row, pivot_row]
        scaled = matrix[pivot_row] / pivot_value[None, :]
        solved = target[pivot_row] / pivot_value
        factors = matrix[:, pivot_row].at[pivot_row].set(0.0)
        matrix = matrix - factors[:, None, :] * scaled[None, :, :]
        matrix = matrix.at[pivot_row].set(scaled)
        target = target - factors * solved[None, :]
        target = target.at[pivot_row].set(solved)
    return target


def reference(stamps, stamp_gain, stamp_invvar, stamp_dest, stamp_obj, phi_tpl, psi_tpl, theta_init, nb_id, nb_weight):
    owner = (stamp_dest[:, 0] * OBJ_DEV + stamp_obj).astype(jnp.int32)
    phi_wide = phi_tpl.astype(jnp.float32)
    psi_wide = psi_tpl.astype(jnp.float32)
    pair = (phi_wide[:, :, None, :] * phi_wide[:, None, :, :]).astype(jnp.bfloat16)
    pair_wide = pair.reshape(BANDS, K * K, PIX).astype(jnp.float32)
    blocks = STAMPS // STAMP_DEV
    stamp_blocks = stamps.reshape(blocks, STAMP_DEV, BANDS, PIX)
    gain_blocks = stamp_gain.reshape(blocks, STAMP_DEV)
    invvar_blocks = stamp_invvar.reshape(blocks, STAMP_DEV)
    owner_blocks = owner.reshape(blocks, STAMP_DEV)
    theta = theta_init
    for sweep in range(ITERS):
        amp = jnp.exp(theta)
        near = jnp.zeros_like(amp)
        for slot_j in range(NEI):
            near = near + nb_weight[:, slot_j][None, :] * jnp.take(amp, nb_id[:, slot_j], axis=1)

        def one_block(carry, inputs):
            normal_acc, grad_acc = carry
            pixels, gains, invvars, owners = inputs
            gain = gains.astype(jnp.float32)
            invvar = invvars.astype(jnp.float32)
            slot_f = jnp.take(amp, owners, axis=1).T
            slot_u = jnp.take(near, owners, axis=1).T
            lit = (gain[:, None] * slot_f).astype(jnp.bfloat16).astype(jnp.float32)
            nearlit = slot_u.astype(jnp.bfloat16).astype(jnp.float32)
            model = jnp.einsum('nk,bkp->nbp', lit, phi_wide) + jnp.einsum('nk,bkp->nbp', nearlit, psi_wide)
            resid = pixels.astype(jnp.float32) - model
            inv_b = invvar[:, None, None]
            weight = inv_b / (1.0 + inv_b * resid * resid / ROBUST)
            weight_low = weight.astype(jnp.bfloat16).astype(jnp.float32)
            wres = (weight * resid).astype(jnp.bfloat16).astype(jnp.float32)
            gram = jnp.einsum('nbp,bmp->nm', weight_low, pair_wide)
            proj = jnp.einsum('nbp,bkp->nk', wres, phi_wide)
            outer = (slot_f[:, :, None] * slot_f[:, None, :]).reshape(slot_f.shape[0], K * K)
            a_rows = (gain * gain)[:, None] * outer * gram
            r_rows = gain[:, None] * slot_f * proj
            normal_acc = normal_acc + jax.ops.segment_sum(a_rows, owners, num_segments=OBJECTS)
            grad_acc = grad_acc + jax.ops.segment_sum(r_rows, owners, num_segments=OBJECTS)
            return (normal_acc, grad_acc), None

        start = (jnp.zeros((OBJECTS, K * K), jnp.float32), jnp.zeros((OBJECTS, K), jnp.float32))
        (normal, grad), unused = lax.scan(one_block, start, (stamp_blocks, gain_blocks, invvar_blocks, owner_blocks))
        matrix = jnp.transpose(normal.reshape(OBJECTS, K, K), (1, 2, 0))
        eye_k = jnp.eye(K, dtype=jnp.float32)[:, :, None]
        matrix = matrix + DAMPING * (matrix * eye_k) + PRIOR * eye_k
        target = grad.T - PRIOR * (theta - theta_init)
        delta = batch_solve(matrix, target)
        theta = theta + STEP_LIMIT * jnp.tanh(delta / STEP_LIMIT)
    return theta
```

```python
import functools

import jax
import jax.numpy as jnp
import numpy as np
from jax import lax
from jax.experimental import pallas as pl
from jax.experimental.pallas import tpu as pltpu
from jax.sharding import PartitionSpec as P

ITERS = 3
CAP = 8
K = 16
ROBUST = 9.0
DAMPING = 0.1
PRIOR = 1.0
STEP_LIMIT = 0.5

MESH = pl.DeviceIdType.MESH
F32 = jnp.float32
BF16 = jnp.bfloat16


def iota(shape, dim):
    return lax.broadcasted_iota(jnp.int32, shape, dim)


def split(x):
    high = x.astype(BF16)
    return high, (x - high.astype(F32)).astype(BF16)


def dot(a, b):
    return jnp.dot(a, b, preferred_element_type=F32)


def dot_t(a, b):
    return lax.dot_general(a, b, (((1,), (1,)), ((), ())), preferred_element_type=F32)


def halves(x):
    width = x.shape[1] // 2
    return x[:, :width] + x[:, width:]


def expand_table():
    table = np.zeros((K * K + K, 384), np.float32)
    for k in range(K):
        for l in range(K):
            a, b = min(k, l), max(k, l)
            if a < 8:
                table[k * K + l, a * K + b] = 1
            elif a == b:
                table[k * K + l, 256 + np.arange(CAP) * K + a - 8] = 1
            else:
                table[k * K + l, (b - 8) * K + a - 8] = 1
        table[K * K + k, 128 + np.arange(CAP) * K + k] = 1
    return table


def solve(full, amp, theta, theta_init):
    sub8 = iota((8, amp.shape[1]), 0)
    amp_lo, amp_hi = amp[:8], amp[8:]
    first, second = [], []
    for k in range(K):
        own = amp[k : k + 1]
        row = full[k * K : k * K + K]
        if k < 8:
            part = row[:8] * (amp_lo * own)
            first.append(part + jnp.where(sub8 == k, DAMPING * part + PRIOR, 0.0))
        else:
            first.append(None)
        part = row[8:] * (amp_hi * own)
        if k >= 8:
            part = part + jnp.where(sub8 == k - 8, DAMPING * part + PRIOR, 0.0)
        second.append(part)
    target = full[K * K :] * amp - PRIOR * (theta - theta_init)
    t0, t1 = target[:8], target[8:]
    ups0, ups1, solved = [], [], []
    for p in range(K):
        r0, r1 = first[p], second[p]
        pivot = r0[p : p + 1] if p < 8 else r1[p - 8 : p - 7]
        inv = 1.0 / pivot
        s0 = None if r0 is None else r0 * inv
        s1 = r1 * inv
        y = (t0[p : p + 1] if p < 8 else t1[p - 8 : p - 7]) * inv
        ups0.append(None if s0 is None else jnp.where(sub8 > p, s0, 0.0))
        ups1.append(jnp.where(sub8 > p - 8, s1, 0.0))
        solved.append(y)
        if r0 is not None:
            t0 = t0 - r0 * y
        t1 = t1 - r1 * y
        for k in range(p + 1, K):
            factor = s0[k : k + 1] if k < 8 else s1[k - 8 : k - 7]
            if k < 8:
                first[k] = first[k] - factor * r0
            second[k] = second[k] - factor * r1
    x0 = jnp.zeros_like(t0)
    x1 = jnp.zeros_like(t1)
    for p in reversed(range(K)):
        known = ups1[p] * x1
        if p < 8:
            known = known + ups0[p] * x0
        value = solved[p] - jnp.sum(known, axis=0, keepdims=True)
        if p < 8:
            x0 = jnp.where(sub8 == p, value, x0)
        else:
            x1 = jnp.where(sub8 == p - 8, value, x1)
    delta = jnp.concatenate([x0, x1], axis=0)
    return theta + STEP_LIMIT * jnp.tanh(delta / STEP_LIMIT)


def kernel(
    dims,
    stamps_ref,
    small_ref,
    nb_ref,
    phi_ref,
    psi_ref,
    theta_ref,
    table_ref,
    out_ref,
    pixels,
    pair,
    wide_phi,
    both,
    gram,
    proj,
    to_slot,
    to_dest,
    from_lit,
    from_near,
    gain_mask,
    plain_mask,
    stamp_cols,
    member,
    member2,
    reply_hi,
    reply_lo,
    theta_now,
    meta_out,
    meta_in,
    nb_in,
    rows_out,
    rows_in,
    reply_out,
    reply_in,
    sums_out,
    sums_in,
    pix_sem,
    meta_send,
    meta_recv,
    nb_send,
    nb_recv,
    rows_send,
    rows_recv,
    reply_send,
    reply_recv,
    sums_send,
    sums_recv,
):
    n_dev, n_stamp, n_obj, pix, chunk = dims
    per_band = pix // chunk
    n_chunk = pixels.shape[0]
    n_slot = n_dev * CAP
    me = lax.axis_index("sky")
    core = lax.axis_index("band")

    def peer(j):
        return lax.rem(me + j, n_dev)

    barrier = pltpu.get_barrier_semaphore()

    def greet(j, carry):
        pl.semaphore_signal(barrier, inc=1, device_id=(peer(j), core), device_id_type=MESH)
        return carry

    lax.fori_loop(1, n_dev, greet, 0)
    pl.semaphore_signal(barrier, inc=1, device_id=(me, 1 - core), device_id_type=MESH)

    pixel_copies = []
    for i in range(n_chunk):
        band, part = divmod(i, per_band)
        copy = pltpu.make_async_copy(
            stamps_ref.at[band, :, pl.ds(part * chunk, chunk)], pixels.at[i], pix_sem.at[i]
        )
        copy.start()
        pixel_copies.append(copy)

    small = small_ref[...]
    cols = jnp.concatenate([small, jnp.zeros((120, n_stamp), F32)], axis=0).T
    gain_row, dest_row, obj_row = small[0:1], small[2:3], small[3:4]
    gain_col, invvar_col, dest_col = cols[:, 0:1], cols[:, 1:2], cols[:, 2:3]
    same = dest_col == dest_row
    low = iota((n_stamp, n_stamp), 0)
    across = iota((n_stamp, n_stamp), 1)
    rank_col = jnp.sum(jnp.where(same & (across < low), 1.0, 0.0), axis=1, keepdims=True)
    rank_row = jnp.sum(jnp.where(same & (low < across), 1.0, 0.0), axis=0, keepdims=True)
    dest_hot = jnp.where(iota((n_dev, n_stamp), 0).astype(F32) == dest_row, 1.0, 0.0).astype(BF16)
    to_dest[...] = dest_hot
    obj_col = cols[:, 3:4]
    named = jnp.where(iota((n_stamp, 128), 1).astype(F32) == rank_col, obj_col + 1.0, 0.0)
    slot_obj = dot(dest_hot, named.astype(BF16))
    meta_out[pl.ds(1, n_dev), 0, :] = slot_obj
    meta_out[0:1, 0, :] = slot_obj[n_dev - 1 :]
    meta_out[n_dev + 1 : n_dev + 2, 0, :] = slot_obj[:1]

    pl.semaphore_wait(barrier, n_dev)

    def send_meta(j, carry):
        t = peer(j)
        pltpu.make_async_remote_copy(
            meta_out.at[pl.ds(t, 3)],
            meta_in.at[:, me],
            meta_send,
            meta_recv,
            device_id=(t, core),
            device_id_type=MESH,
        ).start()
        return carry

    lax.fori_loop(1, n_dev, send_meta, 0)
    nb_copies = []
    for side, step in ((0, 1), (1, n_dev - 1)):
        copy = pltpu.make_async_remote_copy(
            nb_ref,
            nb_in.at[side],
            nb_send.at[side],
            nb_recv.at[side],
            device_id=(peer(step), core),
            device_id_type=MESH,
        )
        copy.start()
        nb_copies.append(copy)
    own_meta = meta_out[pl.ds(me, 3), 0, :]
    meta_in[:, pl.ds(me, 1), 0, :] = own_meta.reshape(3, 1, 128)

    slot_row = dest_row * CAP + rank_row
    to_slot[...] = jnp.where(iota((n_slot, n_stamp), 0).astype(F32) == slot_row, 1.0, 0.0).astype(BF16)
    dest_int = dest_col.astype(jnp.int32)
    owner = iota((n_stamp, n_dev), 1)
    from_lit[...] = jnp.where(owner == dest_int, 1.0, 0.0).astype(BF16)
    shifted = []
    for r in range(3):
        want = dest_int + 1 - r
        want = jnp.where(want < 0, want + n_dev, jnp.where(want >= n_dev, want - n_dev, want))
        shifted.append(jnp.where(owner == want, 1.0, 0.0))
    from_near[...] = jnp.concatenate(shifted, axis=1).astype(BF16)
    group = (iota((n_stamp, 128), 1) // K).astype(F32)
    in_slot = jnp.where(group == rank_col, 1.0, 0.0)
    plain_mask[...] = in_slot
    gain_mask[...] = in_slot * gain_col
    lane = iota((n_stamp, 128), 1)
    stamp_cols[...] = jnp.where(lane == 0, gain_col, jnp.where(lane == 1, ROBUST / invvar_col, 0.0))

    def build(i, carry):
        band = i // per_band
        at = pl.multiple_of((i % per_band) * chunk, chunk)
        phi16 = phi_ref[band, :, pl.ds(at, chunk)]
        phi = phi16.astype(F32)
        swapped = jnp.concatenate([phi[8:], phi[:8]], axis=0)
        sub = iota((K, chunk), 0)
        for k in range(8):
            block = jnp.where(sub >= k, phi * phi[k : k + 1], swapped * phi[8 + k : 9 + k])
            pair[i, k * K : (k + 1) * K, :] = block.astype(BF16)
        rest = (swapped * swapped).astype(BF16)
        for c in range(CAP):
            pair[i, 128 + c * K : 128 + (c + 1) * K, :] = rest
            wide_phi[i, c * K : (c + 1) * K, :] = phi16
        both[i, 0:K, :] = phi16
        both[i, K : 2 * K, :] = psi_ref[band, :, pl.ds(at, chunk)]
        return carry

    for copy in nb_copies:
        copy.wait()
    pltpu.make_async_copy(meta_in.at[:, pl.ds(0, n_dev - 1)], meta_in.at[:, pl.ds(0, n_dev - 1)], meta_recv).wait()
    own_obj = meta_in[1, :, 0, :]
    turned = dot_t(
        jnp.where(iota((128, 128), 0) == iota((128, 128), 1), 1.0, 0.0).astype(BF16), own_obj.astype(BF16)
    )
    spread = dot(
        turned.astype(BF16),
        jnp.where(iota((n_dev, n_slot), 1) // CAP == iota((n_dev, n_slot), 0), 1.0, 0.0).astype(BF16),
    )[:CAP]
    mine = iota((CAP, n_slot), 1) % CAP == iota((CAP, n_slot), 0)
    obj_of_slot = jnp.sum(jnp.where(mine, spread, 0.0), axis=0, keepdims=True)
    member[...] = jnp.where(
        iota((n_obj, n_slot), 0).astype(F32) + 1.0 == obj_of_slot, 1.0, 0.0
    ).astype(BF16)
    obj_sub = iota((n_obj, n_dev), 0).astype(F32) + 1.0
    member2[...] = jnp.concatenate(
        [jnp.where(obj_sub == turned[c : c + 1], 1.0, 0.0) for c in range(CAP)], axis=1
    ).astype(BF16)
    obj_lane = iota((n_dev, n_obj), 1).astype(F32) + 1.0
    reply_hi[0:n_dev, :] = jnp.concatenate(
        [jnp.where(own_obj[:, c : c + 1] == obj_lane, 1.0, 0.0) for c in range(CAP)], axis=1
    ).astype(BF16)
    reply_lo[0:n_dev, :] = jnp.zeros((n_dev, CAP * n_obj), BF16)
    wanted = (iota((n_obj, n_obj), 0) + me * n_obj).astype(F32)
    for r in range(3):
        table = nb_ref[...] if r == 1 else nb_in[0 if r == 0 else 1]
        blend = jnp.zeros((n_obj, n_obj), F32)
        for j in range(4):
            blend = blend + jnp.where(wanted == table[j : j + 1, :n_obj], table[4 + j : 5 + j, :n_obj], 0.0)
        blend_hi, blend_lo = split(blend)
        objects = meta_in[r, :, 0, :]
        his, los = [], []
        for c in range(CAP):
            hot = jnp.where(objects[:, c : c + 1] == obj_lane, 1.0, 0.0).astype(BF16)
            his.append(dot_t(hot, blend_hi))
            los.append(dot_t(hot, blend_lo))
        at = (1 + r) * n_dev
        reply_hi[at : at + n_dev, :] = jnp.concatenate(his, axis=1).astype(BF16)
        reply_lo[at : at + n_dev, :] = jnp.concatenate(los, axis=1).astype(BF16)

    def reply(theta):
        amp = jnp.exp(theta)
        double = jnp.concatenate([amp, amp], axis=1)
        tiled = jnp.concatenate([double] * (CAP // 2), axis=1)
        tiled = jnp.concatenate([tiled] * CAP, axis=0)
        shape = (CAP * K, CAP * n_obj)
        tiled = jnp.where(iota(shape, 0) // K == iota(shape, 1) // n_obj, tiled, 0.0)
        amp_hi, amp_lo = split(tiled)
        answer = (
            dot_t(reply_hi[...], amp_hi) + dot_t(reply_hi[...], amp_lo) + dot_t(reply_lo[...], amp_hi)
        )
        for r in range(4):
            reply_out[r, :, 0, :] = answer[r * n_dev : (r + 1) * n_dev]

        def send(j, carry):
            t = peer(j)
            pltpu.make_async_remote_copy(
                reply_out.at[:, t],
                reply_in.at[:, me],
                reply_send,
                reply_recv,
                device_id=(t, core),
                device_id_type=MESH,
            ).start()
            return carry

        lax.fori_loop(1, n_dev, send, 0)
        reply_in[:, pl.ds(me, 1), 0, :] = reply_out[:, pl.ds(me, 1), 0, :]

    def wait_reply(ref, sem):
        part = ref.at[:, pl.ds(0, n_dev - 1)]
        pltpu.make_async_copy(part, part, sem).wait()

    def wait_rows(ref, sem):
        part = ref.at[pl.ds(0, n_dev - 1)]
        pltpu.make_async_copy(part, part, sem).wait()

    theta_now[...] = theta_ref[...]
    reply(theta_ref[...])
    lax.fori_loop(0, n_chunk, build, 0)
    meta_part = meta_in.at[:, pl.ds(0, n_dev - 1)]
    pltpu.make_async_copy(meta_part, meta_part, meta_send).wait()
    for copy in pixel_copies:
        copy.wait()

    fold_shape = (2 * CAP * K, 2 * K)
    fold_row, fold_col = iota(fold_shape, 0), iota(fold_shape, 1)
    fold = jnp.where(
        (fold_row // (CAP * K) == fold_col // K) & (fold_row % K == fold_col % K), 1.0, 0.0
    ).astype(BF16)

    def sweep(it, carry):
        wait_reply(reply_in, reply_recv)
        lit_hi, lit_lo = split(reply_in[0, :, 0, :])
        near_hi, near_lo = split(jnp.concatenate([reply_in[r, :, 0, :] for r in (1, 2, 3)], axis=0))
        lit = halves(dot(from_lit[...], jnp.concatenate([lit_hi, lit_lo], axis=1)))
        near = halves(dot(from_near[...], jnp.concatenate([near_hi, near_lo], axis=1)))
        wide = jnp.concatenate([lit * gain_mask[...], near * plain_mask[...]], axis=1)
        coeff = dot(wide.astype(BF16), fold).astype(BF16)
        gain = stamp_cols[:, 0:1]
        softening = stamp_cols[:, 1:2]
        gram[...] = jnp.zeros_like(gram)
        proj[...] = jnp.zeros_like(proj)

        def one_chunk(i, carry):
            resid = pixels[i].astype(F32) - dot(coeff, both[i])
            weight = ROBUST / (resid * resid + softening)
            gram[...] += dot_t(weight.astype(BF16), pair[i])
            proj[...] += dot_t((weight * resid).astype(BF16), wide_phi[i])
            return carry

        lax.fori_loop(0, n_chunk, one_chunk, 0)
        square = gain * gain
        main_hi, main_lo = split(gram[:, :128] * square)
        main = halves(dot(to_slot[...], jnp.concatenate([main_hi, main_lo], axis=1)))
        rest = jnp.concatenate(
            [proj[...] * gain_mask[...], gram[:, 128:] * (gain_mask[...] * gain)], axis=1
        )
        rest_hi, rest_lo = split(rest)
        rest = dot(to_dest[...], rest_hi) + dot(to_dest[...], rest_lo)

        @pl.when(it > 0)
        def _():
            wait_rows(rows_out, rows_send)

        rows_out[:, 0:CAP, :] = main.reshape(n_dev, CAP, 128)
        rows_out[:, CAP, :] = rest[:, :128]
        rows_out[:, CAP + 1, :] = rest[:, 128:]

        def send(j, carry):
            t = peer(j)
            pltpu.make_async_remote_copy(
                rows_out.at[t],
                rows_in.at[me],
                rows_send,
                rows_recv,
                device_id=(t, core),
                device_id_type=MESH,
            ).start()
            return carry

        lax.fori_loop(1, n_dev, send, 0)
        rows_in[me] = rows_out[me]

        wait_rows(rows_in, rows_recv)
        slot_hi, slot_lo = split(rows_in[:, 0:CAP, :].reshape(n_slot, 128))
        main_sum = halves(dot(member[...], jnp.concatenate([slot_hi, slot_lo], axis=1)))
        rest = jnp.concatenate([rows_in[:, CAP, :], rows_in[:, CAP + 1, :]], axis=1)
        rest = jnp.concatenate([rest] * CAP, axis=0)
        shape = (CAP * n_dev, 256)
        rest = jnp.where(iota(shape, 0) // n_dev == (iota(shape, 1) % 128) // K, rest, 0.0)
        rest_hi, rest_lo = split(rest)
        rest_sum = dot(member2[...], rest_hi) + dot(member2[...], rest_lo)
        sums = jnp.concatenate([main_sum, rest_sum], axis=1)
        sums_out[it] = sums
        copy = pltpu.make_async_remote_copy(
            sums_out.at[it],
            sums_in.at[it],
            sums_send.at[it],
            sums_recv.at[it],
            device_id=(me, 1 - core),
            device_id_type=MESH,
        )
        copy.start()
        copy.wait()
        sums_hi, sums_lo = split(sums + sums_in[it])
        full = dot_t(table_ref[...], sums_hi) + dot_t(table_ref[...], sums_lo)
        theta = theta_now[...]
        theta = solve(full, jnp.exp(theta), theta, theta_ref[...])
        theta_now[...] = theta
        wait_reply(reply_out, reply_send)

        @pl.when(it < ITERS - 1)
        def _():
            reply(theta)

        return carry

    lax.fori_loop(0, ITERS, sweep, 0)
    wait_rows(rows_out, rows_send)
    out_ref[...] = theta_now[...]


def local(
    stamps,
    stamp_gain,
    stamp_invvar,
    stamp_dest,
    stamp_obj,
    phi_tpl,
    psi_tpl,
    theta_init,
    nb_id,
    nb_weight,
):
    n_dev = lax.axis_size("sky")
    n_stamp, n_band, pix = stamps.shape
    n_obj = theta_init.shape[1]
    chunk = 768 if pix % 768 == 0 else pix
    n_chunk = n_band * (pix // chunk)
    small = jnp.concatenate(
        [
            stamp_gain.astype(F32)[None],
            stamp_invvar.astype(F32)[None],
            stamp_dest[:, 0].astype(F32)[None],
            stamp_obj.astype(F32)[None],
            jnp.zeros((4, n_stamp), F32),
        ],
        axis=0,
    )
    nb = jnp.concatenate([nb_id.T.astype(F32), nb_weight.T], axis=0)
    nb = jnp.pad(nb, ((0, 0), (0, 128 - n_obj)))
    table = jnp.asarray(expand_table(), BF16)
    vmem = pl.BlockSpec(memory_space=pltpu.VMEM)
    n_slot = n_dev * CAP
    scratch = [
        pltpu.VMEM((n_chunk, n_stamp, chunk), BF16),
        pltpu.VMEM((n_chunk, 256, chunk), BF16),
        pltpu.VMEM((n_chunk, 128, chunk), BF16),
        pltpu.VMEM((n_chunk, 32, chunk), BF16),
        pltpu.VMEM((n_stamp, 256), F32),
        pltpu.VMEM((n_stamp, 128), F32),
        pltpu.VMEM((n_slot, n_stamp), BF16),
        pltpu.VMEM((n_dev, n_stamp), BF16),
        pltpu.VMEM((n_stamp, n_dev), BF16),
        pltpu.VMEM((n_stamp, 3 * n_dev), BF16),
        pltpu.VMEM((n_stamp, 128), F32),
        pltpu.VMEM((n_stamp, 128), F32),
        pltpu.VMEM((n_stamp, 128), F32),
        pltpu.VMEM((n_obj, n_slot), BF16),
        pltpu.VMEM((n_obj, n_slot), BF16),
        pltpu.VMEM((4 * n_dev, CAP * n_obj), BF16),
        pltpu.VMEM((4 * n_dev, CAP * n_obj), BF16),
        pltpu.VMEM((K, n_obj), F32),
        pltpu.VMEM((n_dev + 2, 1, 128), F32),
        pltpu.VMEM((3, n_dev, 1, 128), F32),
        pltpu.VMEM((2, 8, 128), F32),
        pltpu.VMEM((n_dev, CAP + 2, 128), F32),
        pltpu.VMEM((n_dev, CAP + 2, 128), F32),
        pltpu.VMEM((4, n_dev, 1, 128), F32),
        pltpu.VMEM((4, n_dev, 1, 128), F32),
        pltpu.VMEM((ITERS, n_obj, 384), F32),
        pltpu.VMEM((ITERS, n_obj, 384), F32),
        pltpu.SemaphoreType.DMA((n_chunk,)),
        pltpu.SemaphoreType.DMA,
        pltpu.SemaphoreType.DMA,
        pltpu.SemaphoreType.DMA((2,)),
        pltpu.SemaphoreType.DMA((2,)),
        pltpu.SemaphoreType.DMA,
        pltpu.SemaphoreType.DMA,
        pltpu.SemaphoreType.DMA,
        pltpu.SemaphoreType.DMA,
        pltpu.SemaphoreType.DMA((ITERS,)),
        pltpu.SemaphoreType.DMA((ITERS,)),
    ]
    return pl.pallas_call(
        functools.partial(kernel, (n_dev, n_stamp, n_obj, pix, chunk)),
        out_shape=jax.ShapeDtypeStruct(theta_init.shape, F32),
        in_specs=[pl.BlockSpec(memory_space=pl.ANY)] + [vmem] * 6,
        out_specs=vmem,
        scratch_shapes=scratch,
        compiler_params=pltpu.CompilerParams(
            collective_id=0, has_side_effects=True, vmem_limit_bytes=50 << 20
        ),
    )(jnp.transpose(stamps, (1, 0, 2)), small, nb, phi_tpl, psi_tpl, theta_init, table)


def solution(mesh):
    in_specs = (
        P("sky", "band", None),
        P("sky"),
        P("sky"),
        P("sky", None),
        P("sky"),
        P("band", None, None),
        P("band", None, None),
        P(None, "sky"),
        P("sky", None),
        P("sky", None),
    )
    out_specs = P(None, "sky")
    return jax.shard_map(local, mesh=mesh, in_specs=in_specs, out_specs=out_specs, check_vma=False)
```

```python
import functools

import jax
import jax.numpy as jnp
import numpy as np
from jax import lax
from jax.experimental import pallas as pl
from jax.experimental.pallas import tpu as pltpu
from jax.sharding import PartitionSpec as P

ITERS = 3
CAP = 8
K = 16
ROBUST = 9.0
DAMPING = 0.1
PRIOR = 1.0
STEP_LIMIT = 0.5

MESH = pl.DeviceIdType.MESH
F32 = jnp.float32
BF16 = jnp.bfloat16


def iota(shape, dim):
    return lax.broadcasted_iota(jnp.int32, shape, dim)


def split(x):
    high = x.astype(BF16)
    return high, (x - high.astype(F32)).astype(BF16)


def dot(a, b):
    return jnp.dot(a, b, preferred_element_type=F32)


def dot_t(a, b):
    return lax.dot_general(a, b, (((1,), (1,)), ((), ())), preferred_element_type=F32)


def halves(x):
    width = x.shape[1] // 2
    return x[:, :width] + x[:, width:]


def expand_table():
    table = np.zeros((K * K + K, 384), np.float32)
    for k in range(K):
        for l in range(K):
            a, b = min(k, l), max(k, l)
            if a < 8:
                table[k * K + l, a * K + b] = 1
            elif a == b:
                table[k * K + l, 256 + np.arange(CAP) * K + a - 8] = 1
            else:
                table[k * K + l, (b - 8) * K + a - 8] = 1
        table[K * K + k, 128 + np.arange(CAP) * K + k] = 1
    return table


def offsets(side):
    steps = [(x, y, z) for x in range(side) for y in range(side) for z in range(side)]
    return sorted(steps[1:], key=lambda s: -sum(min(d, side - d) for d in s))


def solve(full, amp, theta, theta_init):
    sub8 = iota((8, amp.shape[1]), 0)
    amp_lo, amp_hi = amp[:8], amp[8:]
    first, second = [], []
    for k in range(K):
        own = amp[k : k + 1]
        row = full[k * K : k * K + K]
        if k < 8:
            part = row[:8] * (amp_lo * own)
            first.append(part + jnp.where(sub8 == k, DAMPING * part + PRIOR, 0.0))
        else:
            first.append(None)
        part = row[8:] * (amp_hi * own)
        if k >= 8:
            part = part + jnp.where(sub8 == k - 8, DAMPING * part + PRIOR, 0.0)
        second.append(part)
    target = full[K * K :] * amp - PRIOR * (theta - theta_init)
    t0, t1 = target[:8], target[8:]
    ups0, ups1, solved = [], [], []
    for p in range(K):
        r0, r1 = first[p], second[p]
        pivot = r0[p : p + 1] if p < 8 else r1[p - 8 : p - 7]
        inv = 1.0 / pivot
        s0 = None if r0 is None else r0 * inv
        s1 = r1 * inv
        y = (t0[p : p + 1] if p < 8 else t1[p - 8 : p - 7]) * inv
        ups0.append(None if s0 is None else jnp.where(sub8 > p, s0, 0.0))
        ups1.append(jnp.where(sub8 > p - 8, s1, 0.0))
        solved.append(y)
        if r0 is not None:
            t0 = t0 - r0 * y
        t1 = t1 - r1 * y
        for k in range(p + 1, K):
            factor = s0[k : k + 1] if k < 8 else s1[k - 8 : k - 7]
            if k < 8:
                first[k] = first[k] - factor * r0
            second[k] = second[k] - factor * r1
    x0 = jnp.zeros_like(t0)
    x1 = jnp.zeros_like(t1)
    for p in reversed(range(K)):
        known = ups1[p] * x1
        if p < 8:
            known = known + ups0[p] * x0
        value = solved[p] - jnp.sum(known, axis=0, keepdims=True)
        if p < 8:
            x0 = jnp.where(sub8 == p, value, x0)
        else:
            x1 = jnp.where(sub8 == p - 8, value, x1)
    delta = jnp.concatenate([x0, x1], axis=0)
    return theta + STEP_LIMIT * jnp.tanh(delta / STEP_LIMIT)


def kernel(
    dims,
    stamps_ref,
    gain_hbm,
    invvar_hbm,
    dest_hbm,
    obj_hbm,
    phi_hbm,
    psi_hbm,
    theta_hbm,
    nb_id_hbm,
    nb_weight_hbm,
    table_hbm,
    out_ref,
    gain_ref,
    invvar_ref,
    dest_ref,
    obj_ref,
    phi_ref,
    psi_ref,
    theta_ref,
    nb_id_ref,
    nb_weight_ref,
    table_ref,
    nb_ref,
    pixels,
    pair,
    wide_phi,
    both,
    gram,
    proj,
    to_slot,
    to_dest,
    from_lit,
    from_near,
    gain_mask,
    plain_mask,
    stamp_cols,
    member,
    member2,
    reply_hi,
    reply_lo,
    theta_now,
    meta_out,
    meta_in,
    nb_in,
    rows_out,
    rows_in,
    reply_out,
    reply_in,
    sums_out,
    sums_in,
    in_sem,
    pix_sem,
    meta_send,
    meta_recv,
    nb_send,
    nb_recv,
    rows_send,
    rows_recv,
    reply_send,
    reply_recv,
    sums_send,
    sums_recv,
):
    n_dev, n_stamp, n_obj, pix, chunk = dims
    per_band = pix // chunk
    n_chunk = pixels.shape[0]
    n_slot = n_dev * CAP
    me = lax.axis_index("sky")
    core = lax.axis_index("band")

    def peer(j):
        return lax.rem(me + j, n_dev)

    side = 4
    x, y, z = me // (side * side), lax.rem(me // side, side), lax.rem(me, side)
    along_x = [lax.rem(x + d, side) * (side * side) for d in range(side)]
    along_y = [lax.rem(y + d, side) * side for d in range(side)]
    along_z = [lax.rem(z + d, side) for d in range(side)]

    def each_peer(act):
        if n_dev == side**3:
            for dx, dy, dz in offsets(side):
                act(along_x[dx] + along_y[dy] + along_z[dz])
        else:

            def step(j, carry):
                act(peer(j))
                return carry

            lax.fori_loop(1, n_dev, step, 0)

    in_copies = []
    for i, (src, dst) in enumerate(
        (
            (gain_hbm, gain_ref),
            (invvar_hbm, invvar_ref),
            (dest_hbm, dest_ref),
            (obj_hbm, obj_ref),
            (nb_id_hbm, nb_id_ref),
            (nb_weight_hbm, nb_weight_ref),
            (theta_hbm, theta_ref),
            (table_hbm, table_ref),
            (phi_hbm, phi_ref),
            (psi_hbm, psi_ref),
        )
    ):
        copy = pltpu.make_async_copy(src, dst, in_sem.at[i])
        copy.start()
        in_copies.append(copy)
    barrier = pltpu.get_barrier_semaphore()

    def greet(t):
        pl.semaphore_signal(barrier, inc=1, device_id=(t, core), device_id_type=MESH)

    each_peer(greet)
    pl.semaphore_signal(barrier, inc=1, device_id=(me, 1 - core), device_id_type=MESH)

    pixel_copies = []
    for i in range(n_chunk):
        band, part = divmod(i, per_band)
        copy = pltpu.make_async_copy(
            stamps_ref.at[band, :, pl.ds(part * chunk, chunk)], pixels.at[i], pix_sem.at[i]
        )
        copy.start()
        pixel_copies.append(copy)

    for copy in in_copies[:8]:
        copy.wait()
    small = jnp.concatenate(
        [
            gain_ref[...].astype(F32).reshape(1, n_stamp),
            invvar_ref[...].astype(F32).reshape(1, n_stamp),
            dest_ref[...].astype(F32).reshape(1, n_stamp),
            obj_ref[...].astype(F32).reshape(1, n_stamp),
            jnp.zeros((4, n_stamp), F32),
        ],
        axis=0,
    )
    nb_ref[...] = jnp.zeros_like(nb_ref)
    nb_ref[0:4, 0:n_obj] = nb_id_ref[...].astype(F32)
    nb_ref[4:8, 0:n_obj] = nb_weight_ref[...]
    cols = jnp.concatenate([small, jnp.zeros((120, n_stamp), F32)], axis=0).T
    gain_row, dest_row, obj_row = small[0:1], small[2:3], small[3:4]
    gain_col, invvar_col, dest_col = cols[:, 0:1], cols[:, 1:2], cols[:, 2:3]
    same = dest_col == dest_row
    low = iota((n_stamp, n_stamp), 0)
    across = iota((n_stamp, n_stamp), 1)
    rank_col = jnp.sum(jnp.where(same & (across < low), 1.0, 0.0), axis=1, keepdims=True)
    rank_row = jnp.sum(jnp.where(same & (low < across), 1.0, 0.0), axis=0, keepdims=True)
    dest_hot = jnp.where(iota((n_dev, n_stamp), 0).astype(F32) == dest_row, 1.0, 0.0).astype(BF16)
    to_dest[...] = dest_hot
    obj_col = cols[:, 3:4]
    named = jnp.where(iota((n_stamp, 128), 1).astype(F32) == rank_col, obj_col + 1.0, 0.0)
    slot_obj = dot(dest_hot, named.astype(BF16))
    meta_out[pl.ds(1, n_dev), 0, :] = slot_obj
    meta_out[0:1, 0, :] = slot_obj[n_dev - 1 :]
    meta_out[n_dev + 1 : n_dev + 2, 0, :] = slot_obj[:1]

    pl.semaphore_wait(barrier, n_dev)

    def send_meta(t):
        pltpu.make_async_remote_copy(
            meta_out.at[pl.ds(t, 3)],
            meta_in.at[:, me],
            meta_send,
            meta_recv,
            device_id=(t, core),
            device_id_type=MESH,
        ).start()

    each_peer(send_meta)
    nb_copies = []
    for side, step in ((0, 1), (1, n_dev - 1)):
        copy = pltpu.make_async_remote_copy(
            nb_ref,
            nb_in.at[side],
            nb_send.at[side],
            nb_recv.at[side],
            device_id=(peer(step), core),
            device_id_type=MESH,
        )
        copy.start()
        nb_copies.append(copy)
    own_meta = meta_out[pl.ds(me, 3), 0, :]
    meta_in[:, pl.ds(me, 1), 0, :] = own_meta.reshape(3, 1, 128)

    slot_row = dest_row * CAP + rank_row
    to_slot[...] = jnp.where(iota((n_slot, n_stamp), 0).astype(F32) == slot_row, 1.0, 0.0).astype(BF16)
    dest_int = dest_col.astype(jnp.int32)
    owner = iota((n_stamp, n_dev), 1)
    from_lit[...] = jnp.where(owner == dest_int, 1.0, 0.0).astype(BF16)
    shifted = []
    for r in range(3):
        want = dest_int + 1 - r
        want = jnp.where(want < 0, want + n_dev, jnp.where(want >= n_dev, want - n_dev, want))
        shifted.append(jnp.where(owner == want, 1.0, 0.0))
    from_near[...] = jnp.concatenate(shifted, axis=1).astype(BF16)
    group = (iota((n_stamp, 128), 1) // K).astype(F32)
    in_slot = jnp.where(group == rank_col, 1.0, 0.0)
    plain_mask[...] = in_slot
    gain_mask[...] = in_slot * gain_col
    lane = iota((n_stamp, 128), 1)
    stamp_cols[...] = jnp.where(lane == 0, gain_col, jnp.where(lane == 1, ROBUST / invvar_col, 0.0))

    def build(i, carry):
        band = i // per_band
        at = pl.multiple_of((i % per_band) * chunk, chunk)
        phi16 = phi_ref[band, :, pl.ds(at, chunk)]
        phi = phi16.astype(F32)
        swapped = jnp.concatenate([phi[8:], phi[:8]], axis=0)
        sub = iota((K, chunk), 0)
        for k in range(8):
            block = jnp.where(sub >= k, phi * phi[k : k + 1], swapped * phi[8 + k : 9 + k])
            pair[i, k * K : (k + 1) * K, :] = block.astype(BF16)
        rest = (swapped * swapped).astype(BF16)
        for c in range(CAP):
            pair[i, 128 + c * K : 128 + (c + 1) * K, :] = rest
            wide_phi[i, c * K : (c + 1) * K, :] = phi16
        both[i, 0:K, :] = phi16
        both[i, K : 2 * K, :] = psi_ref[band, :, pl.ds(at, chunk)]
        return carry

    for copy in nb_copies:
        copy.wait()
    pltpu.make_async_copy(meta_in.at[:, pl.ds(0, n_dev - 1)], meta_in.at[:, pl.ds(0, n_dev - 1)], meta_recv).wait()
    own_obj = meta_in[1, :, 0, :]
    turned = dot_t(
        jnp.where(iota((128, 128), 0) == iota((128, 128), 1), 1.0, 0.0).astype(BF16), own_obj.astype(BF16)
    )
    spread = dot(
        turned.astype(BF16),
        jnp.where(iota((n_dev, n_slot), 1) // CAP == iota((n_dev, n_slot), 0), 1.0, 0.0).astype(BF16),
    )[:CAP]
    mine = iota((CAP, n_slot), 1) % CAP == iota((CAP, n_slot), 0)
    obj_of_slot = jnp.sum(jnp.where(mine, spread, 0.0), axis=0, keepdims=True)
    member[...] = jnp.where(
        iota((n_obj, n_slot), 0).astype(F32) + 1.0 == obj_of_slot, 1.0, 0.0
    ).astype(BF16)
    obj_sub = iota((n_obj, n_dev), 0).astype(F32) + 1.0
    member2[...] = jnp.concatenate(
        [jnp.where(obj_sub == turned[c : c + 1], 1.0, 0.0) for c in range(CAP)], axis=1
    ).astype(BF16)
    obj_lane = iota((n_dev, n_obj), 1).astype(F32) + 1.0
    reply_hi[0:n_dev, :] = jnp.concatenate(
        [jnp.where(own_obj[:, c : c + 1] == obj_lane, 1.0, 0.0) for c in range(CAP)], axis=1
    ).astype(BF16)
    reply_lo[0:n_dev, :] = jnp.zeros((n_dev, CAP * n_obj), BF16)
    wanted = (iota((n_obj, n_obj), 0) + me * n_obj).astype(F32)
    for r in range(3):
        table = nb_ref[...] if r == 1 else nb_in[0 if r == 0 else 1]
        blend = jnp.zeros((n_obj, n_obj), F32)
        for j in range(4):
            blend = blend + jnp.where(wanted == table[j : j + 1, :n_obj], table[4 + j : 5 + j, :n_obj], 0.0)
        blend_hi, blend_lo = split(blend)
        objects = meta_in[r, :, 0, :]
        his, los = [], []
        for c in range(CAP):
            hot = jnp.where(objects[:, c : c + 1] == obj_lane, 1.0, 0.0).astype(BF16)
            his.append(dot_t(hot, blend_hi))
            los.append(dot_t(hot, blend_lo))
        at = (1 + r) * n_dev
        reply_hi[at : at + n_dev, :] = jnp.concatenate(his, axis=1).astype(BF16)
        reply_lo[at : at + n_dev, :] = jnp.concatenate(los, axis=1).astype(BF16)

    def reply(theta):
        amp = jnp.exp(theta)
        double = jnp.concatenate([amp, amp], axis=1)
        tiled = jnp.concatenate([double] * (CAP // 2), axis=1)
        tiled = jnp.concatenate([tiled] * CAP, axis=0)
        shape = (CAP * K, CAP * n_obj)
        tiled = jnp.where(iota(shape, 0) // K == iota(shape, 1) // n_obj, tiled, 0.0)
        amp_hi, amp_lo = split(tiled)
        answer = (
            dot_t(reply_hi[...], amp_hi) + dot_t(reply_hi[...], amp_lo) + dot_t(reply_lo[...], amp_hi)
        )
        for r in range(4):
            reply_out[r, :, 0, :] = answer[r * n_dev : (r + 1) * n_dev]

        def send(t):
            pltpu.make_async_remote_copy(
                reply_out.at[:, t],
                reply_in.at[:, me],
                reply_send,
                reply_recv,
                device_id=(t, core),
                device_id_type=MESH,
            ).start()

        each_peer(send)
        reply_in[:, pl.ds(me, 1), 0, :] = reply_out[:, pl.ds(me, 1), 0, :]

    def wait_reply(ref, sem):
        part = ref.at[:, pl.ds(0, n_dev - 1)]
        pltpu.make_async_copy(part, part, sem).wait()

    def wait_rows(ref, sem):
        part = ref.at[pl.ds(0, n_dev - 1)]
        pltpu.make_async_copy(part, part, sem).wait()

    theta_now[...] = theta_ref[...]
    reply(theta_ref[...])
    for copy in in_copies[8:]:
        copy.wait()
    lax.fori_loop(0, n_chunk, build, 0)
    meta_part = meta_in.at[:, pl.ds(0, n_dev - 1)]
    pltpu.make_async_copy(meta_part, meta_part, meta_send).wait()
    for copy in pixel_copies:
        copy.wait()

    fold_shape = (2 * CAP * K, 2 * K)
    fold_row, fold_col = iota(fold_shape, 0), iota(fold_shape, 1)
    fold = jnp.where(
        (fold_row // (CAP * K) == fold_col // K) & (fold_row % K == fold_col % K), 1.0, 0.0
    ).astype(BF16)

    def sweep(it, carry):
        wait_reply(reply_in, reply_recv)
        lit_hi, lit_lo = split(reply_in[0, :, 0, :])
        near_hi, near_lo = split(jnp.concatenate([reply_in[r, :, 0, :] for r in (1, 2, 3)], axis=0))
        lit = halves(dot(from_lit[...], jnp.concatenate([lit_hi, lit_lo], axis=1)))
        near = halves(dot(from_near[...], jnp.concatenate([near_hi, near_lo], axis=1)))
        wide = jnp.concatenate([lit * gain_mask[...], near * plain_mask[...]], axis=1)
        coeff = dot(wide.astype(BF16), fold).astype(BF16)
        gain = stamp_cols[:, 0:1]
        softening = stamp_cols[:, 1:2]
        gram[...] = jnp.zeros_like(gram)
        proj[...] = jnp.zeros_like(proj)

        def one_chunk(i, carry):
            resid = pixels[i].astype(F32) - dot(coeff, both[i])
            weight = ROBUST / (resid * resid + softening)
            gram[...] += dot_t(weight.astype(BF16), pair[i])
            proj[...] += dot_t((weight * resid).astype(BF16), wide_phi[i])
            return carry

        lax.fori_loop(0, n_chunk, one_chunk, 0)
        square = gain * gain
        main_hi, main_lo = split(gram[:, :128] * square)
        main = halves(dot(to_slot[...], jnp.concatenate([main_hi, main_lo], axis=1)))
        rest = jnp.concatenate(
            [proj[...] * gain_mask[...], gram[:, 128:] * (gain_mask[...] * gain)], axis=1
        )
        rest_hi, rest_lo = split(rest)
        rest = dot(to_dest[...], rest_hi) + dot(to_dest[...], rest_lo)

        @pl.when(it > 0)
        def _():
            wait_rows(rows_out, rows_send)

        rows_out[:, 0:CAP, :] = main.reshape(n_dev, CAP, 128)
        rows_out[:, CAP, :] = rest[:, :128]
        rows_out[:, CAP + 1, :] = rest[:, 128:]

        def send(t):
            pltpu.make_async_remote_copy(
                rows_out.at[t],
                rows_in.at[me],
                rows_send,
                rows_recv,
                device_id=(t, core),
                device_id_type=MESH,
            ).start()

        each_peer(send)
        rows_in[me] = rows_out[me]

        wait_rows(rows_in, rows_recv)
        slot_hi, slot_lo = split(rows_in[:, 0:CAP, :].reshape(n_slot, 128))
        main_sum = halves(dot(member[...], jnp.concatenate([slot_hi, slot_lo], axis=1)))
        rest = jnp.concatenate([rows_in[:, CAP, :], rows_in[:, CAP + 1, :]], axis=1)
        rest = jnp.concatenate([rest] * CAP, axis=0)
        shape = (CAP * n_dev, 256)
        rest = jnp.where(iota(shape, 0) // n_dev == (iota(shape, 1) % 128) // K, rest, 0.0)
        rest_hi, rest_lo = split(rest)
        rest_sum = dot(member2[...], rest_hi) + dot(member2[...], rest_lo)
        sums = jnp.concatenate([main_sum, rest_sum], axis=1)
        sums_out[it] = sums
        copy = pltpu.make_async_remote_copy(
            sums_out.at[it],
            sums_in.at[it],
            sums_send.at[it],
            sums_recv.at[it],
            device_id=(me, 1 - core),
            device_id_type=MESH,
        )
        copy.start()
        copy.wait()
        sums_hi, sums_lo = split(sums + sums_in[it])
        full = dot_t(table_ref[...], sums_hi) + dot_t(table_ref[...], sums_lo)
        theta = theta_now[...]
        theta = solve(full, jnp.exp(theta), theta, theta_ref[...])
        theta_now[...] = theta
        wait_reply(reply_out, reply_send)

        @pl.when(it < ITERS - 1)
        def _():
            reply(theta)

        return carry

    lax.fori_loop(0, ITERS, sweep, 0)
    wait_rows(rows_out, rows_send)
    out_ref[...] = theta_now[...]


def local(
    stamps,
    stamp_gain,
    stamp_invvar,
    stamp_dest,
    stamp_obj,
    phi_tpl,
    psi_tpl,
    theta_init,
    nb_id,
    nb_weight,
):
    n_dev = lax.axis_size("sky")
    n_stamp, n_band, pix = stamps.shape
    n_obj = theta_init.shape[1]
    chunk = pix
    n_chunk = n_band * (pix // chunk)
    table = jnp.asarray(expand_table(), BF16)
    n_slot = n_dev * CAP
    operands = (
        jnp.transpose(stamps, (1, 0, 2)),
        stamp_gain,
        stamp_invvar,
        stamp_dest.reshape(1, n_stamp),
        stamp_obj.reshape(1, n_stamp),
        phi_tpl,
        psi_tpl,
        theta_init,
        nb_id.T,
        nb_weight.T,
        table,
    )
    scratch = [pltpu.VMEM(a.shape, a.dtype) for a in operands[1:]] + [
        pltpu.VMEM((8, 128), F32),
        pltpu.VMEM((n_chunk, n_stamp, chunk), BF16),
        pltpu.VMEM((n_chunk, 256, chunk), BF16),
        pltpu.VMEM((n_chunk, 128, chunk), BF16),
        pltpu.VMEM((n_chunk, 32, chunk), BF16),
        pltpu.VMEM((n_stamp, 256), F32),
        pltpu.VMEM((n_stamp, 128), F32),
        pltpu.VMEM((n_slot, n_stamp), BF16),
        pltpu.VMEM((n_dev, n_stamp), BF16),
        pltpu.VMEM((n_stamp, n_dev), BF16),
        pltpu.VMEM((n_stamp, 3 * n_dev), BF16),
        pltpu.VMEM((n_stamp, 128), F32),
        pltpu.VMEM((n_stamp, 128), F32),
        pltpu.VMEM((n_stamp, 128), F32),
        pltpu.VMEM((n_obj, n_slot), BF16),
        pltpu.VMEM((n_obj, n_slot), BF16),
        pltpu.VMEM((4 * n_dev, CAP * n_obj), BF16),
        pltpu.VMEM((4 * n_dev, CAP * n_obj), BF16),
        pltpu.VMEM((K, n_obj), F32),
        pltpu.VMEM((n_dev + 2, 1, 128), F32),
        pltpu.VMEM((3, n_dev, 1, 128), F32),
        pltpu.VMEM((2, 8, 128), F32),
        pltpu.VMEM((n_dev, CAP + 2, 128), F32),
        pltpu.VMEM((n_dev, CAP + 2, 128), F32),
        pltpu.VMEM((4, n_dev, 1, 128), F32),
        pltpu.VMEM((4, n_dev, 1, 128), F32),
        pltpu.VMEM((ITERS, n_obj, 384), F32),
        pltpu.VMEM((ITERS, n_obj, 384), F32),
        pltpu.SemaphoreType.DMA((10,)),
        pltpu.SemaphoreType.DMA((n_chunk,)),
        pltpu.SemaphoreType.DMA,
        pltpu.SemaphoreType.DMA,
        pltpu.SemaphoreType.DMA((2,)),
        pltpu.SemaphoreType.DMA((2,)),
        pltpu.SemaphoreType.DMA,
        pltpu.SemaphoreType.DMA,
        pltpu.SemaphoreType.DMA,
        pltpu.SemaphoreType.DMA,
        pltpu.SemaphoreType.DMA((ITERS,)),
        pltpu.SemaphoreType.DMA((ITERS,)),
    ]
    return pl.pallas_call(
        functools.partial(kernel, (n_dev, n_stamp, n_obj, pix, chunk)),
        out_shape=jax.ShapeDtypeStruct(theta_init.shape, F32),
        in_specs=[pl.BlockSpec(memory_space=pltpu.HBM)] * len(operands),
        out_specs=pl.BlockSpec(memory_space=pltpu.VMEM),
        scratch_shapes=scratch,
        compiler_params=pltpu.CompilerParams(
            collective_id=0, has_side_effects=True, vmem_limit_bytes=(64 << 20) - (1 << 16)
        ),
    )(*operands)


def solution(mesh):
    in_specs = (
        P("sky", "band", None),
        P("sky"),
        P("sky"),
        P("sky", None),
        P("sky"),
        P("band", None, None),
        P("band", None, None),
        P(None, "sky"),
        P("sky", None),
        P("sky", None),
    )
    out_specs = P(None, "sky")
    return jax.shard_map(local, mesh=mesh, in_specs=in_specs, out_specs=out_specs, check_vma=False)
```

```python
import functools

import jax
import jax.numpy as jnp
import numpy as np
from jax import lax
from jax.experimental import pallas as pl
from jax.experimental.pallas import tpu as pltpu
from jax.sharding import PartitionSpec as P

ITERS = 3
CAP = 8
K = 16
ROBUST = 9.0
DAMPING = 0.1
PRIOR = 1.0
STEP_LIMIT = 0.5

MESH = pl.DeviceIdType.MESH
F32 = jnp.float32
BF16 = jnp.bfloat16


def iota(shape, dim):
    return lax.broadcasted_iota(jnp.int32, shape, dim)


def split(x):
    high = x.astype(BF16)
    return high, (x - high.astype(F32)).astype(BF16)


def split3(x):
    high, rest = x.astype(BF16), x - x.astype(BF16).astype(F32)
    middle = rest.astype(BF16)
    return high, middle, (rest - middle.astype(F32)).astype(BF16)


def dot(a, b):
    return jnp.dot(a, b, preferred_element_type=F32)


def dot_t(a, b):
    return lax.dot_general(a, b, (((1,), (1,)), ((), ())), preferred_element_type=F32)


def halves(x):
    width = x.shape[1] // 2
    return x[:, :width] + x[:, width:]


def expand_table():
    table = np.zeros((K * K + K, 384), np.float32)
    for k in range(K):
        for l in range(K):
            a, b = min(k, l), max(k, l)
            if a < 8:
                table[k * K + l, a * K + b] = 1
            elif a == b:
                table[k * K + l, 256 + np.arange(CAP) * K + a - 8] = 1
            else:
                table[k * K + l, (b - 8) * K + a - 8] = 1
        table[K * K + k, 128 + np.arange(CAP) * K + k] = 1
    return table


def offsets(side):
    steps = [(x, y, z) for x in range(side) for y in range(side) for z in range(side)]
    return sorted(steps[1:], key=lambda s: -sum(min(d, side - d) for d in s))


def solve(full, amp, theta, theta_init):
    sub8 = iota((8, amp.shape[1]), 0)
    amp_lo, amp_hi = amp[:8], amp[8:]
    first, second = [], []
    for k in range(K):
        own = amp[k : k + 1]
        row = full[k * K : k * K + K]
        if k < 8:
            part = row[:8] * (amp_lo * own)
            first.append(part + jnp.where(sub8 == k, DAMPING * part + PRIOR, 0.0))
        else:
            first.append(None)
        part = row[8:] * (amp_hi * own)
        if k >= 8:
            part = part + jnp.where(sub8 == k - 8, DAMPING * part + PRIOR, 0.0)
        second.append(part)
    target = full[K * K :] * amp - PRIOR * (theta - theta_init)
    t0, t1 = target[:8], target[8:]
    ups0, ups1, solved = [], [], []
    for p in range(K):
        r0, r1 = first[p], second[p]
        pivot = r0[p : p + 1] if p < 8 else r1[p - 8 : p - 7]
        inv = 1.0 / pivot
        s0 = None if r0 is None else r0 * inv
        s1 = r1 * inv
        y = (t0[p : p + 1] if p < 8 else t1[p - 8 : p - 7]) * inv
        ups0.append(None if s0 is None else jnp.where(sub8 > p, s0, 0.0))
        ups1.append(jnp.where(sub8 > p - 8, s1, 0.0))
        solved.append(y)
        if r0 is not None:
            t0 = t0 - r0 * y
        t1 = t1 - r1 * y
        for k in range(p + 1, K):
            factor = s0[k : k + 1] if k < 8 else s1[k - 8 : k - 7]
            if k < 8:
                first[k] = first[k] - factor * r0
            second[k] = second[k] - factor * r1
    x0 = jnp.zeros_like(t0)
    x1 = jnp.zeros_like(t1)
    for p in reversed(range(K)):
        known = ups1[p] * x1
        if p < 8:
            known = known + ups0[p] * x0
        value = solved[p] - jnp.sum(known, axis=0, keepdims=True)
        if p < 8:
            x0 = jnp.where(sub8 == p, value, x0)
        else:
            x1 = jnp.where(sub8 == p - 8, value, x1)
    delta = jnp.concatenate([x0, x1], axis=0)
    return theta + STEP_LIMIT * jnp.tanh(delta / STEP_LIMIT)


def kernel(
    dims,
    stamps_ref,
    gain_hbm,
    invvar_hbm,
    dest_hbm,
    obj_hbm,
    phi_hbm,
    psi_hbm,
    theta_hbm,
    nb_id_hbm,
    nb_weight_hbm,
    table_hbm,
    out_ref,
    gain_ref,
    invvar_ref,
    dest_ref,
    obj_ref,
    phi_ref,
    psi_ref,
    theta_ref,
    nb_id_ref,
    nb_weight_ref,
    table_ref,
    nb_ref,
    pixels,
    pair,
    wide_phi,
    both,
    gram,
    proj,
    to_slot,
    to_dest,
    from_lit,
    from_near,
    gain_mask,
    plain_mask,
    stamp_cols,
    member,
    member2,
    reply_hi,
    reply_lo,
    reply_mask,
    amp_parts,
    theta_now,
    meta_out,
    meta_in,
    nb_in,
    rows_out,
    rows_in,
    reply_out,
    reply_in,
    sums_out,
    sums_in,
    in_sem,
    pix_sem,
    meta_send,
    meta_recv,
    nb_send,
    nb_recv,
    rows_send,
    rows_recv,
    reply_send,
    reply_recv,
    sums_send,
    sums_recv,
):
    n_dev, n_stamp, n_obj, pix, chunk = dims
    per_band = pix // chunk
    n_chunk = pixels.shape[0]
    n_slot = n_dev * CAP
    me = lax.axis_index("sky")
    core = lax.axis_index("band")

    def peer(j):
        return lax.rem(me + j, n_dev)

    side = 4
    x, y, z = me // (side * side), lax.rem(me // side, side), lax.rem(me, side)
    along_x = [lax.rem(x + d, side) * (side * side) for d in range(side)]
    along_y = [lax.rem(y + d, side) * side for d in range(side)]
    along_z = [lax.rem(z + d, side) for d in range(side)]

    def each_peer(act):
        if n_dev == side**3:
            for dx, dy, dz in offsets(side):
                act(along_x[dx] + along_y[dy] + along_z[dz])
        else:

            def step(j, carry):
                act(peer(j))
                return carry

            lax.fori_loop(1, n_dev, step, 0)

    barrier = pltpu.get_barrier_semaphore()

    def greet(t):
        pl.semaphore_signal(barrier, inc=1, device_id=(t, core), device_id_type=MESH)

    each_peer(greet)
    pl.semaphore_signal(barrier, inc=1, device_id=(me, 1 - core), device_id_type=MESH)

    in_copies = []
    for i, (src, dst) in enumerate(
        (
            (gain_hbm, gain_ref),
            (invvar_hbm, invvar_ref),
            (dest_hbm, dest_ref),
            (obj_hbm, obj_ref),
            (nb_id_hbm, nb_id_ref),
            (nb_weight_hbm, nb_weight_ref),
            (theta_hbm, theta_ref),
            (table_hbm, table_ref),
            (phi_hbm, phi_ref),
            (psi_hbm, psi_ref),
        )
    ):
        copy = pltpu.make_async_copy(src, dst, in_sem.at[i])
        copy.start()
        in_copies.append(copy)
    pixel_copies = []
    for i in range(n_chunk):
        band, part = divmod(i, per_band)
        copy = pltpu.make_async_copy(
            stamps_ref.at[band, :, pl.ds(part * chunk, chunk)], pixels.at[i], pix_sem.at[i]
        )
        copy.start()
        pixel_copies.append(copy)

    for copy in in_copies[:8]:
        copy.wait()
    small = jnp.concatenate(
        [
            gain_ref[...].astype(F32).reshape(1, n_stamp),
            invvar_ref[...].astype(F32).reshape(1, n_stamp),
            dest_ref[...].astype(F32).reshape(1, n_stamp),
            obj_ref[...].astype(F32).reshape(1, n_stamp),
            jnp.zeros((4, n_stamp), F32),
        ],
        axis=0,
    )
    nb_ref[...] = jnp.zeros_like(nb_ref)
    nb_ref[0:4, 0:n_obj] = nb_id_ref[...].astype(F32)
    nb_ref[4:8, 0:n_obj] = nb_weight_ref[...]
    cols = jnp.concatenate([small, jnp.zeros((120, n_stamp), F32)], axis=0).T
    gain_row, dest_row, obj_row = small[0:1], small[2:3], small[3:4]
    gain_col, invvar_col, dest_col = cols[:, 0:1], cols[:, 1:2], cols[:, 2:3]
    same = dest_col == dest_row
    low = iota((n_stamp, n_stamp), 0)
    across = iota((n_stamp, n_stamp), 1)
    rank_col = jnp.sum(jnp.where(same & (across < low), 1.0, 0.0), axis=1, keepdims=True)
    rank_row = jnp.sum(jnp.where(same & (low < across), 1.0, 0.0), axis=0, keepdims=True)
    dest_hot = jnp.where(iota((n_dev, n_stamp), 0).astype(F32) == dest_row, 1.0, 0.0).astype(BF16)
    to_dest[...] = dest_hot
    obj_col = cols[:, 3:4]
    named = jnp.where(iota((n_stamp, 128), 1).astype(F32) == rank_col, obj_col + 1.0, 0.0)
    slot_obj = dot(dest_hot, named.astype(BF16))
    meta_out[1 : n_dev + 1] = slot_obj
    meta_out[0:1] = slot_obj[n_dev - 1 :]
    meta_out[n_dev + 1 : n_dev + 2] = slot_obj[:1]

    pl.semaphore_wait(barrier, n_dev)

    nb_copies = []
    for side, step in ((0, 1), (1, n_dev - 1)):
        copy = pltpu.make_async_remote_copy(
            nb_ref,
            nb_in.at[side],
            nb_send.at[side],
            nb_recv.at[side],
            device_id=(peer(step), core),
            device_id_type=MESH,
        )
        copy.start()
        nb_copies.append(copy)
    def send_meta(t):
        pltpu.make_async_remote_copy(
            meta_out.at[pl.ds(t, 3)],
            meta_in.at[:, me],
            meta_send,
            meta_recv,
            device_id=(t, core),
            device_id_type=MESH,
        ).start()

    each_peer(send_meta)
    for r in range(3):
        meta_in[r, pl.ds(me, 1), :] = meta_out[pl.ds(me + r, 1), :]

    slot_row = dest_row * CAP + rank_row
    to_slot[...] = jnp.where(iota((n_slot, n_stamp), 0).astype(F32) == slot_row, 1.0, 0.0).astype(BF16)
    dest_int = dest_col.astype(jnp.int32)
    owner = iota((n_stamp, n_dev), 1)
    from_lit[...] = jnp.where(owner == dest_int, 1.0, 0.0).astype(BF16)
    shifted = []
    for r in range(3):
        want = dest_int + 1 - r
        want = jnp.where(want < 0, want + n_dev, jnp.where(want >= n_dev, want - n_dev, want))
        shifted.append(jnp.where(owner == want, 1.0, 0.0))
    from_near[...] = jnp.concatenate(shifted, axis=1).astype(BF16)
    group = (iota((n_stamp, 128), 1) // K).astype(F32)
    in_slot = jnp.where(group == rank_col, 1.0, 0.0)
    plain_mask[...] = in_slot
    gain_mask[...] = in_slot * gain_col
    lane = iota((n_stamp, 128), 1)
    stamp_cols[...] = jnp.where(lane == 0, gain_col, jnp.where(lane == 1, ROBUST / invvar_col, 0.0))

    def build(i, carry):
        band = i // per_band
        at = pl.multiple_of((i % per_band) * chunk, chunk)
        phi16 = phi_ref[band, :, pl.ds(at, chunk)]
        phi = phi16.astype(F32)
        swapped = jnp.concatenate([phi[8:], phi[:8]], axis=0)
        sub = iota((K, chunk), 0)
        for k in range(8):
            block = jnp.where(sub >= k, phi * phi[k : k + 1], swapped * phi[8 + k : 9 + k])
            pair[i, k * K : (k + 1) * K, :] = block.astype(BF16)
        rest = (swapped * swapped).astype(BF16)
        for c in range(CAP):
            pair[i, 128 + c * K : 128 + (c + 1) * K, :] = rest
            wide_phi[i, c * K : (c + 1) * K, :] = phi16
        both[i, 0:K, :] = phi16
        both[i, K : 2 * K, :] = psi_ref[band, :, pl.ds(at, chunk)]
        return carry

    pairs = CAP // 2
    shape = (CAP * K, CAP * n_obj)
    reply_mask[...] = jnp.where(iota(shape, 0) // K == iota(shape, 1) // n_obj, 1.0, 0.0).astype(BF16)

    def spread_amp(theta):
        for part, amp in enumerate(split3(jnp.exp(theta))):
            double = jnp.concatenate([amp, amp], axis=1)
            tiled = jnp.concatenate([double] * pairs, axis=1)
            amp_parts[part] = jnp.concatenate([tiled] * CAP, axis=0) * reply_mask[...]

    spread_amp(theta_ref[...])
    wanted = (iota((n_obj, n_obj), 0) + me * n_obj).astype(F32)

    def blend_of(table):
        blend = jnp.zeros((n_obj, n_obj), F32)
        for j in range(4):
            blend = blend + jnp.where(wanted == table[j : j + 1, :n_obj], table[4 + j : 5 + j, :n_obj], 0.0)
        zero = jnp.zeros_like(blend)
        twice = jnp.concatenate(
            [jnp.concatenate([blend, zero], axis=1), jnp.concatenate([zero, blend], axis=1)], axis=0
        )
        return jnp.concatenate(split(twice), axis=0)

    blends = [None, blend_of(nb_ref[...]), None]
    for copy in nb_copies:
        copy.wait()
    blends[0], blends[2] = blend_of(nb_in[0]), blend_of(nb_in[1])
    meta_part = meta_in.at[:, pl.ds(0, n_dev - 1)]
    pltpu.make_async_copy(meta_part, meta_part, meta_recv).wait()
    lane = iota((n_dev, 2 * n_obj), 1)
    number = (lane % n_obj).astype(F32) + 1.0
    for r in range(3):
        objects = meta_in[r]
        hots = [
            jnp.where(
                jnp.where(lane < n_obj, objects[:, 2 * i : 2 * i + 1], objects[:, 2 * i + 1 : 2 * i + 2]) == number,
                1.0,
                0.0,
            ).astype(BF16)
            for i in range(pairs)
        ]
        if r == 1:
            reply_hi[0:n_dev, :] = jnp.concatenate(hots, axis=1)
        weights = dot_t(jnp.concatenate(hots, axis=0), blends[r]).astype(BF16)
        at = (1 + r) * n_dev
        for i in range(pairs):
            own = weights[i * n_dev : (i + 1) * n_dev]
            columns = slice(i * 2 * n_obj, (i + 1) * 2 * n_obj)
            reply_hi[at : at + n_dev, columns] = own[:, : 2 * n_obj]
            reply_lo[at - n_dev : at, columns] = own[:, 2 * n_obj :]

    def reply():
        for part in range(3):
            term = dot_t(reply_hi[0:n_dev, :], amp_parts[part])
            lit = term if part == 0 else lit + term
        reply_out[0] = lit
        near = dot_t(reply_hi[n_dev:, :], amp_parts[0]) + dot_t(reply_hi[n_dev:, :], amp_parts[1])
        near = near + dot_t(reply_lo[...], amp_parts[0])
        for r in range(3):
            reply_out[1 + r] = near[r * n_dev : (r + 1) * n_dev]

        def send(t):
            pltpu.make_async_remote_copy(
                reply_out.at[:, pl.ds(t, 1)],
                reply_in.at[:, pl.ds(me, 1)],
                reply_send,
                reply_recv,
                device_id=(t, core),
                device_id_type=MESH,
            ).start()

        each_peer(send)
        reply_in[:, pl.ds(me, 1), :] = reply_out[:, pl.ds(me, 1), :]

    def wait_reply(ref, sem):
        part = ref.at[:, pl.ds(0, n_dev - 1)]
        pltpu.make_async_copy(part, part, sem).wait()

    def wait_rows(ref, sem):
        part = ref.at[pl.ds(0, n_dev - 1)]
        pltpu.make_async_copy(part, part, sem).wait()

    theta_now[...] = theta_ref[...]
    reply()
    own_obj = meta_in[1]
    turned = dot_t(
        jnp.where(iota((128, 128), 0) == iota((128, 128), 1), 1.0, 0.0).astype(BF16), own_obj.astype(BF16)
    )
    placed = dot(
        turned.astype(BF16),
        jnp.where(iota((n_dev, n_slot), 1) // CAP == iota((n_dev, n_slot), 0), 1.0, 0.0).astype(BF16),
    )[:CAP]
    mine = iota((CAP, n_slot), 1) % CAP == iota((CAP, n_slot), 0)
    obj_of_slot = jnp.sum(jnp.where(mine, placed, 0.0), axis=0, keepdims=True)
    member[...] = jnp.where(
        iota((n_obj, n_slot), 0).astype(F32) + 1.0 == obj_of_slot, 1.0, 0.0
    ).astype(BF16)
    obj_sub = iota((n_obj, n_dev), 0).astype(F32) + 1.0
    member2[...] = jnp.concatenate(
        [jnp.where(obj_sub == turned[c : c + 1], 1.0, 0.0) for c in range(CAP)], axis=1
    ).astype(BF16)
    for copy in in_copies[8:]:
        copy.wait()
    lax.fori_loop(0, n_chunk, build, 0)
    pltpu.make_async_copy(meta_part, meta_part, meta_send).wait()
    for copy in pixel_copies:
        copy.wait()

    fold_shape = (2 * CAP * K, 2 * K)
    fold_row, fold_col = iota(fold_shape, 0), iota(fold_shape, 1)
    fold = jnp.where(
        (fold_row // (CAP * K) == fold_col // K) & (fold_row % K == fold_col % K), 1.0, 0.0
    ).astype(BF16)

    def sweep(it, carry):
        wait_reply(reply_in, reply_recv)
        near_hi, near_lo = split(jnp.concatenate([reply_in[r] for r in (1, 2, 3)], axis=0))
        lit = dot(from_lit[...], jnp.concatenate(split3(reply_in[0]), axis=1))
        lit = lit[:, :128] + lit[:, 128:256] + lit[:, 256:]
        near = halves(dot(from_near[...], jnp.concatenate([near_hi, near_lo], axis=1)))
        wide = jnp.concatenate([lit * gain_mask[...], near * plain_mask[...]], axis=1)
        coeff = dot(wide.astype(BF16), fold).astype(BF16)
        gain = stamp_cols[:, 0:1]
        softening = stamp_cols[:, 1:2]
        gram[...] = jnp.zeros_like(gram)
        proj[...] = jnp.zeros_like(proj)

        def one_chunk(i):
            resid = pixels[i].astype(F32) - dot(coeff, both[i])
            weight = ROBUST / (resid * resid + softening)
            gram[...] += dot_t(weight.astype(BF16), pair[i])
            proj[...] += dot_t((weight * resid).astype(BF16), wide_phi[i])

        for i in range(n_chunk):
            one_chunk(i)
        square = gain * gain
        main_hi, main_lo = split(gram[:, :128] * square)
        main = halves(dot(to_slot[...], jnp.concatenate([main_hi, main_lo], axis=1)))
        rest = jnp.concatenate(
            [proj[...] * gain_mask[...], gram[:, 128:] * (gain_mask[...] * gain)], axis=1
        )
        rest_hi, rest_lo = split(rest)
        rest = dot(to_dest[...], rest_hi) + dot(to_dest[...], rest_lo)

        @pl.when(it > 0)
        def _():
            wait_rows(rows_out, rows_send)

        rows_out[:, 0:CAP, :] = main.reshape(n_dev, CAP, 128)
        rows_out[:, CAP, :] = rest[:, :128]
        rows_out[:, CAP + 1, :] = rest[:, 128:]

        def send(t):
            pltpu.make_async_remote_copy(
                rows_out.at[t],
                rows_in.at[me],
                rows_send,
                rows_recv,
                device_id=(t, core),
                device_id_type=MESH,
            ).start()

        each_peer(send)
        rows_in[me] = rows_out[me]

        wait_rows(rows_in, rows_recv)
        slot_hi, slot_lo = split(rows_in[:, 0:CAP, :].reshape(n_slot, 128))
        main_sum = halves(dot(member[...], jnp.concatenate([slot_hi, slot_lo], axis=1)))
        rest = jnp.concatenate([rows_in[:, CAP, :], rows_in[:, CAP + 1, :]], axis=1)
        rest = jnp.concatenate([rest] * CAP, axis=0)
        shape = (CAP * n_dev, 256)
        rest = jnp.where(iota(shape, 0) // n_dev == (iota(shape, 1) % 128) // K, rest, 0.0)
        rest_hi, rest_lo = split(rest)
        rest_sum = dot(member2[...], rest_hi) + dot(member2[...], rest_lo)
        sums = jnp.concatenate([main_sum, rest_sum], axis=1)
        sums_out[it] = sums
        copy = pltpu.make_async_remote_copy(
            sums_out.at[it],
            sums_in.at[it],
            sums_send.at[it],
            sums_recv.at[it],
            device_id=(me, 1 - core),
            device_id_type=MESH,
        )
        copy.start()
        copy.wait()
        sums_hi, sums_lo = split(sums + sums_in[it])
        full = dot_t(table_ref[...], sums_hi) + dot_t(table_ref[...], sums_lo)
        theta = theta_now[...]
        theta = solve(full, jnp.exp(theta), theta, theta_ref[...])
        theta_now[...] = theta
        wait_reply(reply_out, reply_send)

        @pl.when(it < ITERS - 1)
        def _():
            spread_amp(theta)
            reply()

        return carry

    lax.fori_loop(0, ITERS, sweep, 0)
    wait_rows(rows_out, rows_send)
    out_ref[...] = theta_now[...]


def local(
    stamps,
    stamp_gain,
    stamp_invvar,
    stamp_dest,
    stamp_obj,
    phi_tpl,
    psi_tpl,
    theta_init,
    nb_id,
    nb_weight,
):
    n_dev = lax.axis_size("sky")
    n_stamp, n_band, pix = stamps.shape
    n_obj = theta_init.shape[1]
    chunk = pix
    n_chunk = n_band * (pix // chunk)
    table = jnp.asarray(expand_table(), BF16)
    n_slot = n_dev * CAP
    operands = (
        jnp.transpose(stamps, (1, 0, 2)),
        stamp_gain,
        stamp_invvar,
        stamp_dest.reshape(1, n_stamp),
        stamp_obj.reshape(1, n_stamp),
        phi_tpl,
        psi_tpl,
        theta_init,
        nb_id.T,
        nb_weight.T,
        table,
    )
    scratch = [pltpu.VMEM(a.shape, a.dtype) for a in operands[1:]] + [
        pltpu.VMEM((8, 128), F32),
        pltpu.VMEM((n_chunk, n_stamp, chunk), BF16),
        pltpu.VMEM((n_chunk, 256, chunk), BF16),
        pltpu.VMEM((n_chunk, 128, chunk), BF16),
        pltpu.VMEM((n_chunk, 32, chunk), BF16),
        pltpu.VMEM((n_stamp, 256), F32),
        pltpu.VMEM((n_stamp, 128), F32),
        pltpu.VMEM((n_slot, n_stamp), BF16),
        pltpu.VMEM((n_dev, n_stamp), BF16),
        pltpu.VMEM((n_stamp, n_dev), BF16),
        pltpu.VMEM((n_stamp, 3 * n_dev), BF16),
        pltpu.VMEM((n_stamp, 128), F32),
        pltpu.VMEM((n_stamp, 128), F32),
        pltpu.VMEM((n_stamp, 128), F32),
        pltpu.VMEM((n_obj, n_slot), BF16),
        pltpu.VMEM((n_obj, n_slot), BF16),
        pltpu.VMEM((4 * n_dev, CAP * n_obj), BF16),
        pltpu.VMEM((3 * n_dev, CAP * n_obj), BF16),
        pltpu.VMEM((CAP * K, CAP * n_obj), BF16),
        pltpu.VMEM((3, CAP * K, CAP * n_obj), BF16),
        pltpu.VMEM((K, n_obj), F32),
        pltpu.VMEM((n_dev + 8, 128), F32),
        pltpu.VMEM((3, n_dev, 128), F32),
        pltpu.VMEM((2, 8, 128), F32),
        pltpu.VMEM((n_dev, CAP + 2, 128), F32),
        pltpu.VMEM((n_dev, CAP + 2, 128), F32),
        pltpu.VMEM((4, n_dev, 128), F32),
        pltpu.VMEM((4, n_dev, 128), F32),
        pltpu.VMEM((ITERS, n_obj, 384), F32),
        pltpu.VMEM((ITERS, n_obj, 384), F32),
        pltpu.SemaphoreType.DMA((10,)),
        pltpu.SemaphoreType.DMA((n_chunk,)),
        pltpu.SemaphoreType.DMA,
        pltpu.SemaphoreType.DMA,
        pltpu.SemaphoreType.DMA((2,)),
        pltpu.SemaphoreType.DMA((2,)),
        pltpu.SemaphoreType.DMA,
        pltpu.SemaphoreType.DMA,
        pltpu.SemaphoreType.DMA,
        pltpu.SemaphoreType.DMA,
        pltpu.SemaphoreType.DMA((ITERS,)),
        pltpu.SemaphoreType.DMA((ITERS,)),
    ]
    return pl.pallas_call(
        functools.partial(kernel, (n_dev, n_stamp, n_obj, pix, chunk)),
        out_shape=jax.ShapeDtypeStruct(theta_init.shape, F32),
        in_specs=[pl.BlockSpec(memory_space=pltpu.HBM)] * len(operands),
        out_specs=pl.BlockSpec(memory_space=pltpu.VMEM),
        scratch_shapes=scratch,
        compiler_params=pltpu.CompilerParams(
            collective_id=0, has_side_effects=True, vmem_limit_bytes=(64 << 20) - (1 << 16)
        ),
    )(*operands)


def solution(mesh):
    in_specs = (
        P("sky", "band", None),
        P("sky"),
        P("sky"),
        P("sky", None),
        P("sky"),
        P("band", None, None),
        P("band", None, None),
        P(None, "sky"),
        P("sky", None),
        P("sky", None),
    )
    out_specs = P(None, "sky")
    return jax.shard_map(local, mesh=mesh, in_specs=in_specs, out_specs=out_specs, check_vma=False)
```

```python
import functools

import jax
import jax.numpy as jnp
import numpy as np
from jax import lax
from jax.experimental import pallas as pl
from jax.experimental.pallas import tpu as pltpu
from jax.sharding import PartitionSpec as P

ITERS = 3
CAP = 8
K = 16
ROBUST = 9.0
DAMPING = 0.1
PRIOR = 1.0
STEP_LIMIT = 0.5

MESH = pl.DeviceIdType.MESH
F32 = jnp.float32
BF16 = jnp.bfloat16


def iota(shape, dim):
    return lax.broadcasted_iota(jnp.int32, shape, dim)


def split(x):
    high = x.astype(BF16)
    return high, (x - high.astype(F32)).astype(BF16)


def split3(x):
    high, rest = x.astype(BF16), x - x.astype(BF16).astype(F32)
    middle = rest.astype(BF16)
    return high, middle, (rest - middle.astype(F32)).astype(BF16)


def dot(a, b):
    return jnp.dot(a, b, preferred_element_type=F32)


def dot_t(a, b):
    return lax.dot_general(a, b, (((1,), (1,)), ((), ())), preferred_element_type=F32)


def halves(x):
    width = x.shape[1] // 2
    return x[:, :width] + x[:, width:]


def expand_table():
    table = np.zeros((K * K + K, 384), np.float32)
    for k in range(K):
        for l in range(K):
            a, b = min(k, l), max(k, l)
            if a < 8:
                table[k * K + l, a * K + b] = 1
            elif a == b:
                table[k * K + l, 256 + np.arange(CAP) * K + a - 8] = 1
            else:
                table[k * K + l, (b - 8) * K + a - 8] = 1
        table[K * K + k, 128 + np.arange(CAP) * K + k] = 1
    return table


def offsets(side):
    steps = [(x, y, z) for x in range(side) for y in range(side) for z in range(side)]
    return sorted(steps[1:], key=lambda s: -sum(min(d, side - d) for d in s))


def solve(full, amp, theta, theta_init):
    sub8 = iota((8, amp.shape[1]), 0)
    amp_lo, amp_hi = amp[:8], amp[8:]
    first, second = [], []
    for k in range(K):
        own = amp[k : k + 1]
        row = full[k * K : k * K + K]
        if k < 8:
            part = row[:8] * (amp_lo * own)
            first.append(part + jnp.where(sub8 == k, DAMPING * part + PRIOR, 0.0))
        else:
            first.append(None)
        part = row[8:] * (amp_hi * own)
        if k >= 8:
            part = part + jnp.where(sub8 == k - 8, DAMPING * part + PRIOR, 0.0)
        second.append(part)
    target = full[K * K :] * amp - PRIOR * (theta - theta_init)
    t0, t1 = target[:8], target[8:]
    ups0, ups1, solved = [], [], []
    for p in range(K):
        r0, r1 = first[p], second[p]
        pivot = r0[p : p + 1] if p < 8 else r1[p - 8 : p - 7]
        inv = 1.0 / pivot
        s0 = None if r0 is None else r0 * inv
        s1 = r1 * inv
        y = (t0[p : p + 1] if p < 8 else t1[p - 8 : p - 7]) * inv
        ups0.append(None if s0 is None else jnp.where(sub8 > p, s0, 0.0))
        ups1.append(jnp.where(sub8 > p - 8, s1, 0.0))
        solved.append(y)
        if r0 is not None:
            t0 = t0 - r0 * y
        t1 = t1 - r1 * y
        for k in range(p + 1, K):
            factor = s0[k : k + 1] if k < 8 else s1[k - 8 : k - 7]
            if k < 8:
                first[k] = first[k] - factor * r0
            second[k] = second[k] - factor * r1
    x0 = jnp.zeros_like(t0)
    x1 = jnp.zeros_like(t1)
    for p in reversed(range(K)):
        known = ups1[p] * x1
        if p < 8:
            known = known + ups0[p] * x0
        value = solved[p] - jnp.sum(known, axis=0, keepdims=True)
        if p < 8:
            x0 = jnp.where(sub8 == p, value, x0)
        else:
            x1 = jnp.where(sub8 == p - 8, value, x1)
    delta = jnp.concatenate([x0, x1], axis=0)
    return STEP_LIMIT * jnp.tanh(delta / STEP_LIMIT)


def kernel(
    dims,
    stamps_ref,
    gain_hbm,
    invvar_hbm,
    dest_hbm,
    obj_hbm,
    phi_hbm,
    psi_hbm,
    theta_hbm,
    nb_id_hbm,
    nb_weight_hbm,
    table_hbm,
    out_ref,
    gain_ref,
    invvar_ref,
    dest_ref,
    obj_ref,
    phi_ref,
    psi_ref,
    theta_ref,
    nb_id_ref,
    nb_weight_ref,
    table_ref,
    nb_ref,
    pixels,
    pair,
    both,
    gram,
    proj,
    to_slot,
    to_dest,
    from_lit,
    from_near,
    gain_mask,
    gain_rows,
    plain_mask,
    stamp_cols,
    member,
    member2,
    reply_hi,
    reply_lo,
    reply_mask,
    amp_parts,
    theta_now,
    meta_out,
    meta_in,
    nb_in,
    rows_out,
    rows_in,
    reply_out,
    reply_in,
    sums_out,
    sums_in,
    in_sem,
    pix_sem,
    meta_send,
    meta_recv,
    nb_send,
    nb_recv,
    rows_send,
    rows_recv,
    reply_send,
    reply_recv,
    sums_send,
    sums_recv,
):
    n_dev, n_stamp, n_obj, pix, chunk = dims
    per_band = pix // chunk
    n_chunk = pixels.shape[0]
    n_slot = n_dev * CAP
    me = lax.axis_index("sky")
    core = lax.axis_index("band")

    def peer(j):
        return lax.rem(me + j, n_dev)

    side = 4
    x, y, z = me // (side * side), lax.rem(me // side, side), lax.rem(me, side)
    along_x = [lax.rem(x + d, side) * (side * side) for d in range(side)]
    along_y = [lax.rem(y + d, side) * side for d in range(side)]
    along_z = [lax.rem(z + d, side) for d in range(side)]

    def each_peer(act):
        if n_dev == side**3:
            for dx, dy, dz in offsets(side):
                act(along_x[dx] + along_y[dy] + along_z[dz])
        else:

            def step(j, carry):
                act(peer(j))
                return carry

            lax.fori_loop(1, n_dev, step, 0)

    barrier = pltpu.get_barrier_semaphore()

    def greet(t):
        pl.semaphore_signal(barrier, inc=1, device_id=(t, core), device_id_type=MESH)

    each_peer(greet)
    pl.semaphore_signal(barrier, inc=1, device_id=(me, 1 - core), device_id_type=MESH)

    in_copies = []
    for i, (src, dst) in enumerate(
        (
            (gain_hbm, gain_ref),
            (invvar_hbm, invvar_ref),
            (dest_hbm, dest_ref),
            (obj_hbm, obj_ref),
            (nb_id_hbm, nb_id_ref),
            (nb_weight_hbm, nb_weight_ref),
            (theta_hbm, theta_ref),
            (table_hbm, table_ref),
            (phi_hbm, phi_ref),
            (psi_hbm, psi_ref),
        )
    ):
        copy = pltpu.make_async_copy(src, dst, in_sem.at[i])
        copy.start()
        in_copies.append(copy)
    pixel_copies = []
    for i in range(n_chunk):
        band, part = divmod(i, per_band)
        copy = pltpu.make_async_copy(
            stamps_ref.at[band, :, pl.ds(part * chunk, chunk)], pixels.at[i], pix_sem.at[i]
        )
        copy.start()
        pixel_copies.append(copy)

    for copy in in_copies[:8]:
        copy.wait()
    small = jnp.concatenate(
        [
            gain_ref[...].astype(F32).reshape(1, n_stamp),
            invvar_ref[...].astype(F32).reshape(1, n_stamp),
            dest_ref[...].astype(F32).reshape(1, n_stamp),
            obj_ref[...].astype(F32).reshape(1, n_stamp),
            jnp.zeros((4, n_stamp), F32),
        ],
        axis=0,
    )
    nb_ref[...] = jnp.zeros_like(nb_ref)
    nb_ref[0:4, 0:n_obj] = nb_id_ref[...].astype(F32)
    nb_ref[4:8, 0:n_obj] = nb_weight_ref[...]
    cols = jnp.concatenate([small, jnp.zeros((120, n_stamp), F32)], axis=0).T
    gain_row, dest_row, obj_row = small[0:1], small[2:3], small[3:4]
    gain_col, invvar_col, dest_col = cols[:, 0:1], cols[:, 1:2], cols[:, 2:3]
    same = dest_col == dest_row
    low = iota((n_stamp, n_stamp), 0)
    across = iota((n_stamp, n_stamp), 1)
    rank_col = jnp.sum(jnp.where(same & (across < low), 1.0, 0.0), axis=1, keepdims=True)
    rank_row = jnp.sum(jnp.where(same & (low < across), 1.0, 0.0), axis=0, keepdims=True)
    dest_hot = jnp.where(iota((n_dev, n_stamp), 0).astype(F32) == dest_row, 1.0, 0.0).astype(BF16)
    to_dest[...] = dest_hot
    obj_col = cols[:, 3:4]
    named = jnp.where(iota((n_stamp, 128), 1).astype(F32) == rank_col, obj_col + 1.0, 0.0)
    slot_obj = dot(dest_hot, named.astype(BF16))
    meta_out[1 : n_dev + 1] = slot_obj
    meta_out[0:1] = slot_obj[n_dev - 1 :]
    meta_out[n_dev + 1 : n_dev + 2] = slot_obj[:1]

    pl.semaphore_wait(barrier, n_dev)

    nb_copies = []
    for side, step in ((0, 1), (1, n_dev - 1)):
        copy = pltpu.make_async_remote_copy(
            nb_ref,
            nb_in.at[side],
            nb_send.at[side],
            nb_recv.at[side],
            device_id=(peer(step), core),
            device_id_type=MESH,
        )
        copy.start()
        nb_copies.append(copy)
    def send_meta(t):
        pltpu.make_async_remote_copy(
            meta_out.at[pl.ds(t, 3)],
            meta_in.at[:, me],
            meta_send,
            meta_recv,
            device_id=(t, core),
            device_id_type=MESH,
        ).start()

    each_peer(send_meta)
    for r in range(3):
        meta_in[r, pl.ds(me, 1), :] = meta_out[pl.ds(me + r, 1), :]

    slot_row = dest_row * CAP + rank_row
    to_slot[...] = jnp.where(iota((n_slot, n_stamp), 0).astype(F32) == slot_row, 1.0, 0.0).astype(BF16)
    dest_int = dest_col.astype(jnp.int32)
    owner = iota((n_stamp, n_dev), 1)
    from_lit[...] = jnp.where(owner == dest_int, 1.0, 0.0).astype(BF16)
    shifted = []
    for r in range(3):
        want = dest_int + 1 - r
        want = jnp.where(want < 0, want + n_dev, jnp.where(want >= n_dev, want - n_dev, want))
        shifted.append(jnp.where(owner == want, 1.0, 0.0))
    from_near[...] = jnp.concatenate(shifted, axis=1).astype(BF16)
    group = (iota((n_stamp, 128), 1) // K).astype(F32)
    in_slot = jnp.where(group == rank_col, 1.0, 0.0)
    plain_mask[...] = in_slot
    gain_mask[...] = in_slot * gain_col
    in_slot_row = (iota((128, n_stamp), 0) // K).astype(F32) == rank_row
    gain_rows[...] = jnp.where(in_slot_row, gain_row, 0.0)
    lane = iota((n_stamp, 128), 1)
    stamp_cols[...] = jnp.where(lane == 0, gain_col, jnp.where(lane == 1, ROBUST / invvar_col, 0.0))

    def build(i, carry):
        band = i // per_band
        at = pl.multiple_of((i % per_band) * chunk, chunk)
        phi16 = phi_ref[band, :, pl.ds(at, chunk)]
        phi = phi16.astype(F32)
        swapped = jnp.concatenate([phi[8:], phi[:8]], axis=0)
        sub = iota((K, chunk), 0)
        for k in range(8):
            block = jnp.where(sub >= k, phi * phi[k : k + 1], swapped * phi[8 + k : 9 + k])
            pair[i, k * K : (k + 1) * K, :] = block.astype(BF16)
        rest = (swapped * swapped).astype(BF16)
        for c in range(CAP):
            pair[i, 128 + c * K : 128 + (c + 1) * K, :] = rest
        both[i, 0:K, :] = phi16
        both[i, K : 2 * K, :] = psi_ref[band, :, pl.ds(at, chunk)]
        return carry

    pairs = CAP // 2
    shape = (CAP * K, CAP * n_obj)
    reply_mask[...] = jnp.where(iota(shape, 0) // K == iota(shape, 1) // n_obj, 1.0, 0.0).astype(BF16)

    def spread_amp(theta):
        for part, amp in enumerate(split3(jnp.exp(theta))):
            double = jnp.concatenate([amp, amp], axis=1)
            tiled = jnp.concatenate([double] * pairs, axis=1)
            amp_parts[part] = jnp.concatenate([tiled] * CAP, axis=0) * reply_mask[...]

    spread_amp(theta_ref[...])
    wanted = (iota((n_obj, n_obj), 0) + me * n_obj).astype(F32)

    def blend_of(table):
        blend = jnp.zeros((n_obj, n_obj), F32)
        for j in range(4):
            blend = blend + jnp.where(wanted == table[j : j + 1, :n_obj], table[4 + j : 5 + j, :n_obj], 0.0)
        zero = jnp.zeros_like(blend)
        twice = jnp.concatenate(
            [jnp.concatenate([blend, zero], axis=1), jnp.concatenate([zero, blend], axis=1)], axis=0
        )
        return jnp.concatenate(split3(twice), axis=0)

    blends = [None, blend_of(nb_ref[...]), None]
    for copy in nb_copies:
        copy.wait()
    blends[0], blends[2] = blend_of(nb_in[0]), blend_of(nb_in[1])
    meta_part = meta_in.at[:, pl.ds(0, n_dev - 1)]
    pltpu.make_async_copy(meta_part, meta_part, meta_recv).wait()
    lane = iota((n_dev, 2 * n_obj), 1)
    number = (lane % n_obj).astype(F32) + 1.0
    for r in range(3):
        objects = meta_in[r]
        hots = [
            jnp.where(
                jnp.where(lane < n_obj, objects[:, 2 * i : 2 * i + 1], objects[:, 2 * i + 1 : 2 * i + 2]) == number,
                1.0,
                0.0,
            ).astype(BF16)
            for i in range(pairs)
        ]
        if r == 1:
            reply_hi[0:n_dev, :] = jnp.concatenate(hots, axis=1)
        weights = dot_t(jnp.concatenate(hots, axis=0), blends[r]).astype(BF16)
        at = (1 + r) * n_dev
        for i in range(pairs):
            own = weights[i * n_dev : (i + 1) * n_dev]
            columns = slice(i * 2 * n_obj, (i + 1) * 2 * n_obj)
            reply_hi[at : at + n_dev, columns] = own[:, : 2 * n_obj]
            reply_lo[0, at - n_dev : at, columns] = own[:, 2 * n_obj : 4 * n_obj]
            reply_lo[1, at - n_dev : at, columns] = own[:, 4 * n_obj :]

    def reply():
        for part in range(3):
            term = dot_t(reply_hi[0:n_dev, :], amp_parts[part])
            lit = term if part == 0 else lit + term
        reply_out[0] = lit
        tables = (reply_hi[n_dev:, :], reply_lo[0], reply_lo[1])
        near = dot_t(tables[2], amp_parts[0]) + dot_t(tables[0], amp_parts[2]) + dot_t(tables[1], amp_parts[1])
        near = near + dot_t(tables[1], amp_parts[0]) + dot_t(tables[0], amp_parts[1])
        near = near + dot_t(tables[0], amp_parts[0])
        for r in range(3):
            reply_out[1 + r] = near[r * n_dev : (r + 1) * n_dev]

        def send(t):
            pltpu.make_async_remote_copy(
                reply_out.at[:, pl.ds(t, 1)],
                reply_in.at[:, pl.ds(me, 1)],
                reply_send,
                reply_recv,
                device_id=(t, core),
                device_id_type=MESH,
            ).start()

        each_peer(send)
        reply_in[:, pl.ds(me, 1), :] = reply_out[:, pl.ds(me, 1), :]

    def wait_reply(ref, sem):
        part = ref.at[:, pl.ds(0, n_dev - 1)]
        pltpu.make_async_copy(part, part, sem).wait()

    def wait_rows(ref, sem):
        part = ref.at[pl.ds(0, n_dev - 1)]
        pltpu.make_async_copy(part, part, sem).wait()

    theta_now[...] = theta_ref[...]
    reply()
    own_obj = meta_in[1]
    turned = dot_t(
        jnp.where(iota((128, 128), 0) == iota((128, 128), 1), 1.0, 0.0).astype(BF16), own_obj.astype(BF16)
    )
    placed = dot(
        turned.astype(BF16),
        jnp.where(iota((n_dev, n_slot), 1) // CAP == iota((n_dev, n_slot), 0), 1.0, 0.0).astype(BF16),
    )[:CAP]
    mine = iota((CAP, n_slot), 1) % CAP == iota((CAP, n_slot), 0)
    obj_of_slot = jnp.sum(jnp.where(mine, placed, 0.0), axis=0, keepdims=True)
    member[...] = jnp.where(
        iota((n_obj, n_slot), 0).astype(F32) + 1.0 == obj_of_slot, 1.0, 0.0
    ).astype(BF16)
    obj_sub = iota((n_obj, n_dev), 0).astype(F32) + 1.0
    member2[...] = jnp.concatenate(
        [jnp.where(obj_sub == turned[c : c + 1], 1.0, 0.0) for c in range(CAP)], axis=1
    ).astype(BF16)
    for copy in in_copies[8:]:
        copy.wait()
    lax.fori_loop(0, n_chunk, build, 0)
    pltpu.make_async_copy(meta_part, meta_part, meta_send).wait()
    for copy in pixel_copies:
        copy.wait()

    fold_shape = (2 * CAP * K, 2 * K)
    fold_row, fold_col = iota(fold_shape, 0), iota(fold_shape, 1)
    fold = jnp.where(
        (fold_row // (CAP * K) == fold_col // K) & (fold_row % K == fold_col % K), 1.0, 0.0
    ).astype(BF16)

    def sweep(it, carry):
        wait_reply(reply_in, reply_recv)
        near = jnp.concatenate([reply_in[r] for r in (1, 2, 3)], axis=0)
        lit = dot(from_lit[...], jnp.concatenate(split3(reply_in[0]), axis=1))
        lit = lit[:, :128] + lit[:, 128:256] + lit[:, 256:]
        near = dot(from_near[...], jnp.concatenate(split3(near), axis=1))
        near = near[:, :128] + near[:, 128:256] + near[:, 256:]
        wide = jnp.concatenate([lit * gain_mask[...], near * plain_mask[...]], axis=1)
        coeff = dot(wide.astype(BF16), fold).astype(BF16)
        gain = stamp_cols[:, 0:1]
        softening = stamp_cols[:, 1:2]
        gram[...] = jnp.zeros_like(gram)
        proj[...] = jnp.zeros_like(proj)

        def one_chunk(i):
            resid = pixels[i].astype(F32) - dot(coeff, both[i])
            weight = ROBUST / (resid * resid + softening)
            gram[...] += dot_t(weight.astype(BF16), pair[i])
            proj[...] += dot_t(both[i, 0:K, :], (weight * resid).astype(BF16))

        for i in range(n_chunk):
            one_chunk(i)
        main_hi, main_lo = split(gram[:, :128] * (gain * gain))
        main = halves(dot(to_slot[...], jnp.concatenate([main_hi, main_lo], axis=1)))
        proj_hi, proj_lo = split(jnp.concatenate([proj[...]] * CAP, axis=0) * gain_rows[...])
        diag_hi, diag_lo = split(gram[:, 128:] * (gain_mask[...] * gain))
        rest_proj = dot_t(to_dest[...], proj_hi) + dot_t(to_dest[...], proj_lo)
        rest_diag = dot(to_dest[...], diag_hi) + dot(to_dest[...], diag_lo)

        @pl.when(it > 0)
        def _():
            wait_rows(rows_out, rows_send)

        rows_out[:, 0:CAP, :] = main.reshape(n_dev, CAP, 128)
        rows_out[:, CAP, :] = rest_proj
        rows_out[:, CAP + 1, :] = rest_diag

        def send(t):
            pltpu.make_async_remote_copy(
                rows_out.at[t],
                rows_in.at[me],
                rows_send,
                rows_recv,
                device_id=(t, core),
                device_id_type=MESH,
            ).start()

        each_peer(send)
        rows_in[me] = rows_out[me]

        wait_rows(rows_in, rows_recv)
        slot_hi, slot_lo = split(rows_in[:, 0:CAP, :].reshape(n_slot, 128))
        main_sum = halves(dot(member[...], jnp.concatenate([slot_hi, slot_lo], axis=1)))
        rest = jnp.concatenate([rows_in[:, CAP, :], rows_in[:, CAP + 1, :]], axis=1)
        rest = jnp.concatenate([rest] * CAP, axis=0)
        shape = (CAP * n_dev, 256)
        rest = jnp.where(iota(shape, 0) // n_dev == (iota(shape, 1) % 128) // K, rest, 0.0)
        rest_hi, rest_lo = split(rest)
        rest_sum = dot(member2[...], rest_hi) + dot(member2[...], rest_lo)
        sums = jnp.concatenate([main_sum, rest_sum], axis=1)
        sums_out[it] = sums
        copy = pltpu.make_async_remote_copy(
            sums_out.at[it],
            sums_in.at[it],
            sums_send.at[it],
            sums_recv.at[it],
            device_id=(me, 1 - core),
            device_id_type=MESH,
        )
        copy.start()
        copy.wait()
        sums_hi, sums_lo = split(sums + sums_in[it])
        full = dot_t(table_ref[...], sums_hi) + dot_t(table_ref[...], sums_lo)
        theta = theta_now[...]
        step = solve(full, jnp.exp(theta), theta, theta_ref[...])
        out_ref[0:K] = theta
        out_ref[K:] = step
        theta = theta + step
        theta_now[...] = theta
        wait_reply(reply_out, reply_send)

        @pl.when(it < ITERS - 1)
        def _():
            spread_amp(theta)
            reply()

        return carry

    lax.fori_loop(0, ITERS, sweep, 0)
    wait_rows(rows_out, rows_send)


def local(
    stamps,
    stamp_gain,
    stamp_invvar,
    stamp_dest,
    stamp_obj,
    phi_tpl,
    psi_tpl,
    theta_init,
    nb_id,
    nb_weight,
):
    n_dev = lax.axis_size("sky")
    n_stamp, n_band, pix = stamps.shape
    n_obj = theta_init.shape[1]
    chunk = pix
    n_chunk = n_band * (pix // chunk)
    table = jnp.asarray(expand_table(), BF16)
    n_slot = n_dev * CAP
    operands = (
        jnp.transpose(stamps, (1, 0, 2)),
        stamp_gain,
        stamp_invvar,
        stamp_dest.reshape(1, n_stamp),
        stamp_obj.reshape(1, n_stamp),
        phi_tpl,
        psi_tpl,
        theta_init,
        nb_id.T,
        nb_weight.T,
        table,
    )
    scratch = [pltpu.VMEM(a.shape, a.dtype) for a in operands[1:]] + [
        pltpu.VMEM((8, 128), F32),
        pltpu.VMEM((n_chunk, n_stamp, chunk), BF16),
        pltpu.VMEM((n_chunk, 256, chunk), BF16),
        pltpu.VMEM((n_chunk, 32, chunk), BF16),
        pltpu.VMEM((n_stamp, 256), F32),
        pltpu.VMEM((K, n_stamp), F32),
        pltpu.VMEM((n_slot, n_stamp), BF16),
        pltpu.VMEM((n_dev, n_stamp), BF16),
        pltpu.VMEM((n_stamp, n_dev), BF16),
        pltpu.VMEM((n_stamp, 3 * n_dev), BF16),
        pltpu.VMEM((n_stamp, 128), F32),
        pltpu.VMEM((128, n_stamp), F32),
        pltpu.VMEM((n_stamp, 128), F32),
        pltpu.VMEM((n_stamp, 128), F32),
        pltpu.VMEM((n_obj, n_slot), BF16),
        pltpu.VMEM((n_obj, n_slot), BF16),
        pltpu.VMEM((4 * n_dev, CAP * n_obj), BF16),
        pltpu.VMEM((2, 3 * n_dev, CAP * n_obj), BF16),
        pltpu.VMEM((CAP * K, CAP * n_obj), BF16),
        pltpu.VMEM((3, CAP * K, CAP * n_obj), BF16),
        pltpu.VMEM((K, n_obj), F32),
        pltpu.VMEM((n_dev + 8, 128), F32),
        pltpu.VMEM((3, n_dev, 128), F32),
        pltpu.VMEM((2, 8, 128), F32),
        pltpu.VMEM((n_dev, CAP + 2, 128), F32),
        pltpu.VMEM((n_dev, CAP + 2, 128), F32),
        pltpu.VMEM((4, n_dev, 128), F32),
        pltpu.VMEM((4, n_dev, 128), F32),
        pltpu.VMEM((ITERS, n_obj, 384), F32),
        pltpu.VMEM((ITERS, n_obj, 384), F32),
        pltpu.SemaphoreType.DMA((10,)),
        pltpu.SemaphoreType.DMA((n_chunk,)),
        pltpu.SemaphoreType.DMA,
        pltpu.SemaphoreType.DMA,
        pltpu.SemaphoreType.DMA((2,)),
        pltpu.SemaphoreType.DMA((2,)),
        pltpu.SemaphoreType.DMA,
        pltpu.SemaphoreType.DMA,
        pltpu.SemaphoreType.DMA,
        pltpu.SemaphoreType.DMA,
        pltpu.SemaphoreType.DMA((ITERS,)),
        pltpu.SemaphoreType.DMA((ITERS,)),
    ]
    fitted = pl.pallas_call(
        functools.partial(kernel, (n_dev, n_stamp, n_obj, pix, chunk)),
        out_shape=jax.ShapeDtypeStruct((2 * K, n_obj), F32),
        in_specs=[pl.BlockSpec(memory_space=pltpu.HBM)] * len(operands),
        out_specs=pl.BlockSpec(memory_space=pltpu.VMEM),
        scratch_shapes=scratch,
        compiler_params=pltpu.CompilerParams(
            collective_id=0, has_side_effects=True, vmem_limit_bytes=(64 << 20) - (1 << 16)
        ),
    )(*operands)
    return fitted[:K] + fitted[K:]


def solution(mesh):
    in_specs = (
        P("sky", "band", None),
        P("sky"),
        P("sky"),
        P("sky", None),
        P("sky"),
        P("band", None, None),
        P("band", None, None),
        P(None, "sky"),
        P("sky", None),
        P("sky", None),
    )
    out_specs = P(None, "sky")
    return jax.shard_map(local, mesh=mesh, in_specs=in_specs, out_specs=out_specs, check_vma=False)
```

```python
import functools

import jax
import jax.numpy as jnp
import numpy as np
from jax import lax
from jax.experimental import pallas as pl
from jax.experimental.pallas import tpu as pltpu
from jax.sharding import PartitionSpec as P

ITERS = 3
CAP = 8
K = 16
ROBUST = 9.0
DAMPING = 0.1
PRIOR = 1.0
STEP_LIMIT = 0.5

MESH = pl.DeviceIdType.MESH
F32 = jnp.float32
BF16 = jnp.bfloat16


def iota(shape, dim):
    return lax.broadcasted_iota(jnp.int32, shape, dim)


def split(x):
    high = x.astype(BF16)
    return high, (x - high.astype(F32)).astype(BF16)


def split3(x):
    high, rest = x.astype(BF16), x - x.astype(BF16).astype(F32)
    middle = rest.astype(BF16)
    return high, middle, (rest - middle.astype(F32)).astype(BF16)


def dot(a, b):
    return jnp.dot(a, b, preferred_element_type=F32)


def dot_t(a, b):
    return lax.dot_general(a, b, (((1,), (1,)), ((), ())), preferred_element_type=F32)


def dot_exact(a, x):
    width = x.shape[1]
    sums = dot(a, jnp.concatenate(split3(x), axis=1))
    return sums[:, :width] + (sums[:, width : 2 * width] + sums[:, 2 * width :])


def dot_close(a, x):
    width = x.shape[1]
    sums = dot(a, jnp.concatenate(split(x), axis=1))
    return sums[:, :width] + sums[:, width:]


def dot_t_exact(a, x):
    high, middle, low = split3(x)
    return dot_t(a, high) + (dot_t(a, middle) + dot_t(a, low))


def expand_table():
    table = np.zeros((K * K + K, 384), np.float32)
    for k in range(K):
        for l in range(K):
            a, b = min(k, l), max(k, l)
            if a < 8:
                table[k * K + l, a * K + b] = 1
            elif a == b:
                table[k * K + l, 256 + np.arange(CAP) * K + a - 8] = 1
            else:
                table[k * K + l, (b - 8) * K + a - 8] = 1
        table[K * K + k, 128 + np.arange(CAP) * K + k] = 1
    return table


def offsets(side):
    steps = [(x, y, z) for x in range(side) for y in range(side) for z in range(side)]
    return sorted(steps[1:], key=lambda s: -sum(min(d, side - d) for d in s))


def solve(full, amp, theta, theta_init):
    sub8 = iota((8, amp.shape[1]), 0)
    amp_lo, amp_hi = amp[:8], amp[8:]
    first, second = [], []
    for k in range(K):
        own = amp[k : k + 1]
        row = full[k * K : k * K + K]
        if k < 8:
            part = row[:8] * (amp_lo * own)
            first.append(part + jnp.where(sub8 == k, DAMPING * part + PRIOR, 0.0))
        else:
            first.append(None)
        part = row[8:] * (amp_hi * own)
        if k >= 8:
            part = part + jnp.where(sub8 == k - 8, DAMPING * part + PRIOR, 0.0)
        second.append(part)
    target = full[K * K :] * amp - PRIOR * (theta - theta_init)
    t0, t1 = target[:8], target[8:]
    ups0, ups1, solved = [], [], []
    for p in range(K):
        r0, r1 = first[p], second[p]
        pivot = r0[p : p + 1] if p < 8 else r1[p - 8 : p - 7]
        inv = 1.0 / pivot
        s0 = None if r0 is None else r0 * inv
        s1 = r1 * inv
        y = (t0[p : p + 1] if p < 8 else t1[p - 8 : p - 7]) * inv
        ups0.append(None if s0 is None else jnp.where(sub8 > p, s0, 0.0))
        ups1.append(jnp.where(sub8 > p - 8, s1, 0.0))
        solved.append(y)
        if r0 is not None:
            t0 = t0 - r0 * y
        t1 = t1 - r1 * y
        for k in range(p + 1, K):
            factor = s0[k : k + 1] if k < 8 else s1[k - 8 : k - 7]
            if k < 8:
                first[k] = first[k] - factor * r0
            second[k] = second[k] - factor * r1
    x0 = jnp.zeros_like(t0)
    x1 = jnp.zeros_like(t1)
    for p in reversed(range(K)):
        known = ups1[p] * x1
        if p < 8:
            known = known + ups0[p] * x0
        value = solved[p] - jnp.sum(known, axis=0, keepdims=True)
        if p < 8:
            x0 = jnp.where(sub8 == p, value, x0)
        else:
            x1 = jnp.where(sub8 == p - 8, value, x1)
    delta = jnp.concatenate([x0, x1], axis=0)
    return STEP_LIMIT * jnp.tanh(delta / STEP_LIMIT)


def kernel(
    dims,
    stamps_ref,
    gain_hbm,
    invvar_hbm,
    dest_hbm,
    obj_hbm,
    phi_hbm,
    psi_hbm,
    theta_hbm,
    nb_id_hbm,
    nb_weight_hbm,
    table_hbm,
    out_ref,
    gain_ref,
    invvar_ref,
    dest_ref,
    obj_ref,
    phi_ref,
    psi_ref,
    theta_ref,
    nb_id_ref,
    nb_weight_ref,
    table_ref,
    nb_ref,
    pixels,
    pair,
    both,
    gram,
    proj,
    to_slot,
    to_dest,
    from_lit,
    from_near,
    gain_mask,
    gain_rows,
    plain_mask,
    stamp_cols,
    member,
    member2,
    reply_hi,
    reply_lo,
    reply_mask,
    rest_mask,
    amp_parts,
    theta_now,
    meta_out,
    meta_in,
    nb_in,
    rows_out,
    rows_in,
    reply_out,
    reply_in,
    sums_out,
    sums_in,
    in_sem,
    pix_sem,
    meta_send,
    meta_recv,
    nb_send,
    nb_recv,
    rows_send,
    rows_recv,
    reply_send,
    reply_recv,
    sums_send,
    sums_recv,
):
    n_dev, n_stamp, n_obj, pix, chunk = dims
    per_band = pix // chunk
    n_chunk = pixels.shape[0]
    n_slot = n_dev * CAP
    me = lax.axis_index("sky")
    core = lax.axis_index("band")

    def peer(j):
        return lax.rem(me + j, n_dev)

    side = 4
    x, y, z = me // (side * side), lax.rem(me // side, side), lax.rem(me, side)
    along_x = [lax.rem(x + d, side) * (side * side) for d in range(side)]
    along_y = [lax.rem(y + d, side) * side for d in range(side)]
    along_z = [lax.rem(z + d, side) for d in range(side)]

    def each_peer(act):
        if n_dev == side**3:
            for dx, dy, dz in offsets(side):
                act(along_x[dx] + along_y[dy] + along_z[dz])
        else:

            def step(j, carry):
                act(peer(j))
                return carry

            lax.fori_loop(1, n_dev, step, 0)

    barrier = pltpu.get_barrier_semaphore()

    def greet(t):
        pl.semaphore_signal(barrier, inc=1, device_id=(t, core), device_id_type=MESH)

    each_peer(greet)
    pl.semaphore_signal(barrier, inc=1, device_id=(me, 1 - core), device_id_type=MESH)

    in_copies = []
    for i, (src, dst) in enumerate(
        (
            (gain_hbm, gain_ref),
            (invvar_hbm, invvar_ref),
            (dest_hbm, dest_ref),
            (obj_hbm, obj_ref),
            (nb_id_hbm, nb_id_ref),
            (nb_weight_hbm, nb_weight_ref),
            (theta_hbm, theta_ref),
            (table_hbm, table_ref),
            (phi_hbm, phi_ref),
            (psi_hbm, psi_ref),
        )
    ):
        copy = pltpu.make_async_copy(src, dst, in_sem.at[i])
        copy.start()
        in_copies.append(copy)
    pixel_copies = []
    for i in range(n_chunk):
        band, part = divmod(i, per_band)
        copy = pltpu.make_async_copy(
            stamps_ref.at[band, :, pl.ds(part * chunk, chunk)], pixels.at[i], pix_sem.at[i]
        )
        copy.start()
        pixel_copies.append(copy)

    for copy in in_copies[:8]:
        copy.wait()
    small = jnp.concatenate(
        [
            gain_ref[...].astype(F32).reshape(1, n_stamp),
            invvar_ref[...].astype(F32).reshape(1, n_stamp),
            dest_ref[...].astype(F32).reshape(1, n_stamp),
            obj_ref[...].astype(F32).reshape(1, n_stamp),
            jnp.zeros((4, n_stamp), F32),
        ],
        axis=0,
    )
    nb_ref[...] = jnp.zeros_like(nb_ref)
    nb_ref[0:4, 0:n_obj] = nb_id_ref[...].astype(F32)
    nb_ref[4:8, 0:n_obj] = nb_weight_ref[...]
    cols = jnp.concatenate([small, jnp.zeros((120, n_stamp), F32)], axis=0).T
    gain_row, dest_row, obj_row = small[0:1], small[2:3], small[3:4]
    gain_col, invvar_col, dest_col = cols[:, 0:1], cols[:, 1:2], cols[:, 2:3]
    same = dest_col == dest_row
    low = iota((n_stamp, n_stamp), 0)
    across = iota((n_stamp, n_stamp), 1)
    rank_col = jnp.sum(jnp.where(same & (across < low), 1.0, 0.0), axis=1, keepdims=True)
    rank_row = jnp.sum(jnp.where(same & (low < across), 1.0, 0.0), axis=0, keepdims=True)
    dest_hot = jnp.where(iota((n_dev, n_stamp), 0).astype(F32) == dest_row, 1.0, 0.0).astype(BF16)
    to_dest[...] = dest_hot
    obj_col = cols[:, 3:4]
    named = jnp.where(iota((n_stamp, 128), 1).astype(F32) == rank_col, obj_col + 1.0, 0.0)
    slot_obj = dot(dest_hot, named.astype(BF16))
    meta_out[1 : n_dev + 1] = slot_obj
    meta_out[0:1] = slot_obj[n_dev - 1 :]
    meta_out[n_dev + 1 : n_dev + 2] = slot_obj[:1]

    pl.semaphore_wait(barrier, n_dev)

    nb_copies = []
    for side, step in ((0, 1), (1, n_dev - 1)):
        copy = pltpu.make_async_remote_copy(
            nb_ref,
            nb_in.at[side],
            nb_send.at[side],
            nb_recv.at[side],
            device_id=(peer(step), core),
            device_id_type=MESH,
        )
        copy.start()
        nb_copies.append(copy)
    def send_meta(t):
        pltpu.make_async_remote_copy(
            meta_out.at[pl.ds(t, 3)],
            meta_in.at[:, me],
            meta_send,
            meta_recv,
            device_id=(t, core),
            device_id_type=MESH,
        ).start()

    each_peer(send_meta)
    for r in range(3):
        meta_in[r, pl.ds(me, 1), :] = meta_out[pl.ds(me + r, 1), :]

    slot_row = dest_row * CAP + rank_row
    to_slot[...] = jnp.where(iota((n_slot, n_stamp), 0).astype(F32) == slot_row, 1.0, 0.0).astype(BF16)
    dest_int = dest_col.astype(jnp.int32)
    owner = iota((n_stamp, n_dev), 1)
    from_lit[...] = jnp.where(owner == dest_int, 1.0, 0.0).astype(BF16)
    shifted = []
    for r in range(3):
        want = dest_int + 1 - r
        want = jnp.where(want < 0, want + n_dev, jnp.where(want >= n_dev, want - n_dev, want))
        shifted.append(jnp.where(owner == want, 1.0, 0.0))
    from_near[...] = jnp.concatenate(shifted, axis=1).astype(BF16)
    group = (iota((n_stamp, 128), 1) // K).astype(F32)
    in_slot = jnp.where(group == rank_col, 1.0, 0.0)
    plain_mask[...] = in_slot
    gain_mask[...] = in_slot * gain_col
    in_slot_row = (iota((128, n_stamp), 0) // K).astype(F32) == rank_row
    gain_rows[...] = jnp.where(in_slot_row, gain_row, 0.0)
    lane = iota((n_stamp, 128), 1)
    stamp_cols[...] = jnp.where(lane == 0, gain_col, jnp.where(lane == 1, ROBUST / invvar_col, 0.0))

    def build(i, carry):
        band = i // per_band
        at = pl.multiple_of((i % per_band) * chunk, chunk)
        phi16 = phi_ref[band, :, pl.ds(at, chunk)]
        phi = phi16.astype(F32)
        swapped = jnp.concatenate([phi[8:], phi[:8]], axis=0)
        sub = iota((K, chunk), 0)
        for k in range(8):
            block = jnp.where(sub >= k, phi * phi[k : k + 1], swapped * phi[8 + k : 9 + k])
            pair[i, k * K : (k + 1) * K, :] = block.astype(BF16)
        rest = (swapped * swapped).astype(BF16)
        for c in range(CAP):
            pair[i, 128 + c * K : 128 + (c + 1) * K, :] = rest
        both[i, 0:K, :] = phi16
        both[i, K : 2 * K, :] = psi_ref[band, :, pl.ds(at, chunk)]
        return carry

    pairs = CAP // 2
    shape = (CAP * K, CAP * n_obj)
    reply_mask[...] = jnp.where(iota(shape, 0) // K == iota(shape, 1) // n_obj, 1.0, 0.0).astype(BF16)

    def spread_amp(theta):
        for part, amp in enumerate(split3(jnp.exp(theta))):
            double = jnp.concatenate([amp, amp], axis=1)
            tiled = jnp.concatenate([double] * pairs, axis=1)
            amp_parts[part] = jnp.concatenate([tiled] * CAP, axis=0) * reply_mask[...]

    spread_amp(theta_ref[...])
    wanted = (iota((n_obj, n_obj), 0) + me * n_obj).astype(F32)

    def blend_of(table):
        blend = jnp.zeros((n_obj, n_obj), F32)
        for j in range(4):
            blend = blend + jnp.where(wanted == table[j : j + 1, :n_obj], table[4 + j : 5 + j, :n_obj], 0.0)
        zero = jnp.zeros_like(blend)
        twice = jnp.concatenate(
            [jnp.concatenate([blend, zero], axis=1), jnp.concatenate([zero, blend], axis=1)], axis=0
        )
        return jnp.concatenate(split3(twice), axis=0)

    blends = [None, blend_of(nb_ref[...]), None]
    for copy in nb_copies:
        copy.wait()
    blends[0], blends[2] = blend_of(nb_in[0]), blend_of(nb_in[1])
    meta_part = meta_in.at[:, pl.ds(0, n_dev - 1)]
    pltpu.make_async_copy(meta_part, meta_part, meta_recv).wait()
    lane = iota((n_dev, 2 * n_obj), 1)
    number = (lane % n_obj).astype(F32) + 1.0
    for r in range(3):
        objects = meta_in[r]
        hots = [
            jnp.where(
                jnp.where(lane < n_obj, objects[:, 2 * i : 2 * i + 1], objects[:, 2 * i + 1 : 2 * i + 2]) == number,
                1.0,
                0.0,
            ).astype(BF16)
            for i in range(pairs)
        ]
        if r == 1:
            reply_hi[0:n_dev, :] = jnp.concatenate(hots, axis=1)
        weights = dot_t(jnp.concatenate(hots, axis=0), blends[r]).astype(BF16)
        at = (1 + r) * n_dev
        for i in range(pairs):
            own = weights[i * n_dev : (i + 1) * n_dev]
            columns = slice(i * 2 * n_obj, (i + 1) * 2 * n_obj)
            reply_hi[at : at + n_dev, columns] = own[:, : 2 * n_obj]
            reply_lo[0, at - n_dev : at, columns] = own[:, 2 * n_obj : 4 * n_obj]
            reply_lo[1, at - n_dev : at, columns] = own[:, 4 * n_obj :]

    def reply():
        for part in range(3):
            term = dot_t(reply_hi[0:n_dev, :], amp_parts[part])
            lit = term if part == 0 else lit + term
        reply_out[0] = lit
        tables = (reply_hi[n_dev:, :], reply_lo[0], reply_lo[1])
        near = dot_t(tables[2], amp_parts[0]) + dot_t(tables[0], amp_parts[2]) + dot_t(tables[1], amp_parts[1])
        near = near + dot_t(tables[1], amp_parts[0]) + dot_t(tables[0], amp_parts[1])
        near = near + dot_t(tables[0], amp_parts[0])
        for r in range(3):
            reply_out[1 + r] = near[r * n_dev : (r + 1) * n_dev]

        def send(t):
            pltpu.make_async_remote_copy(
                reply_out.at[:, pl.ds(t, 1)],
                reply_in.at[:, pl.ds(me, 1)],
                reply_send,
                reply_recv,
                device_id=(t, core),
                device_id_type=MESH,
            ).start()

        each_peer(send)
        reply_in[:, pl.ds(me, 1), :] = reply_out[:, pl.ds(me, 1), :]

    def wait_reply(ref, sem):
        part = ref.at[:, pl.ds(0, n_dev - 1)]
        pltpu.make_async_copy(part, part, sem).wait()

    def wait_rows(ref, sem):
        part = ref.at[pl.ds(0, n_dev - 1)]
        pltpu.make_async_copy(part, part, sem).wait()

    theta_now[...] = theta_ref[...]
    reply()
    shape = (CAP * n_dev, 5 * 128)
    rest_mask[...] = jnp.where(
        iota(shape, 0) // n_dev == (iota(shape, 1) % 128) // K, 1.0, 0.0
    ).astype(BF16)
    own_obj = meta_in[1]
    turned = dot_t(
        jnp.where(iota((128, 128), 0) == iota((128, 128), 1), 1.0, 0.0).astype(BF16), own_obj.astype(BF16)
    )
    placed = dot(
        turned.astype(BF16),
        jnp.where(iota((n_dev, n_slot), 1) // CAP == iota((n_dev, n_slot), 0), 1.0, 0.0).astype(BF16),
    )[:CAP]
    mine = iota((CAP, n_slot), 1) % CAP == iota((CAP, n_slot), 0)
    obj_of_slot = jnp.sum(jnp.where(mine, placed, 0.0), axis=0, keepdims=True)
    member[...] = jnp.where(
        iota((n_obj, n_slot), 0).astype(F32) + 1.0 == obj_of_slot, 1.0, 0.0
    ).astype(BF16)
    obj_sub = iota((n_obj, n_dev), 0).astype(F32) + 1.0
    member2[...] = jnp.concatenate(
        [jnp.where(obj_sub == turned[c : c + 1], 1.0, 0.0) for c in range(CAP)], axis=1
    ).astype(BF16)
    for copy in in_copies[8:]:
        copy.wait()
    lax.fori_loop(0, n_chunk, build, 0)
    pltpu.make_async_copy(meta_part, meta_part, meta_send).wait()
    for copy in pixel_copies:
        copy.wait()

    fold_shape = (2 * CAP * K, 2 * K)
    fold_row, fold_col = iota(fold_shape, 0), iota(fold_shape, 1)
    fold = jnp.where(
        (fold_row // (CAP * K) == fold_col // K) & (fold_row % K == fold_col % K), 1.0, 0.0
    ).astype(BF16)

    def sweep(it, carry):
        wait_reply(reply_in, reply_recv)
        near = jnp.concatenate([reply_in[r] for r in (1, 2, 3)], axis=0)
        lit = dot_exact(from_lit[...], reply_in[0])
        near = dot_exact(from_near[...], near)
        wide = jnp.concatenate([lit * gain_mask[...], near * plain_mask[...]], axis=1)
        coeff = dot(wide.astype(BF16), fold).astype(BF16)
        gain = stamp_cols[:, 0:1]
        softening = stamp_cols[:, 1:2]
        gram[...] = jnp.zeros_like(gram)
        proj[...] = jnp.zeros_like(proj)

        def one_chunk(i):
            resid = pixels[i].astype(F32) - dot(coeff, both[i])
            weight = ROBUST / (resid * resid + softening)
            gram[...] += dot_t(weight.astype(BF16), pair[i])
            proj[...] += dot_t(both[i, 0:K, :], (weight * resid).astype(BF16))

        for i in range(n_chunk):
            one_chunk(i)
        main = dot_close(to_slot[...], gram[:, :128] * (gain * gain))
        rest_proj = dot_t_exact(to_dest[...], jnp.concatenate([proj[...]] * CAP, axis=0) * gain_rows[...])
        rest_diag = dot_close(to_dest[...], gram[:, 128:] * (gain_mask[...] * gain))

        @pl.when(it > 0)
        def _():
            wait_rows(rows_out, rows_send)

        rows_out[:, 0:CAP, :] = main.reshape(n_dev, CAP, 128)
        rows_out[:, CAP, :] = rest_proj
        rows_out[:, CAP + 1, :] = rest_diag

        def send(t):
            pltpu.make_async_remote_copy(
                rows_out.at[t],
                rows_in.at[me],
                rows_send,
                rows_recv,
                device_id=(t, core),
                device_id_type=MESH,
            ).start()

        each_peer(send)
        rows_in[me] = rows_out[me]

        wait_rows(rows_in, rows_recv)
        main_sum = dot_close(member[...], rows_in[:, 0:CAP, :].reshape(n_slot, 128))
        parts = split3(rows_in[:, CAP, :]) + split(rows_in[:, CAP + 1, :])
        parts = jnp.concatenate(parts, axis=1)
        parts = dot(member2[...], jnp.concatenate([parts] * CAP, axis=0) * rest_mask[...])
        proj_sum = parts[:, 0:128] + (parts[:, 128:256] + parts[:, 256:384])
        rest_sum = jnp.concatenate([proj_sum, parts[:, 384:512] + parts[:, 512:640]], axis=1)
        sums = jnp.concatenate([main_sum, rest_sum], axis=1)
        sums_out[it] = sums
        copy = pltpu.make_async_remote_copy(
            sums_out.at[it],
            sums_in.at[it],
            sums_send.at[it],
            sums_recv.at[it],
            device_id=(me, 1 - core),
            device_id_type=MESH,
        )
        copy.start()
        copy.wait()
        full = dot_t_exact(table_ref[...], sums + sums_in[it])
        theta = theta_now[...]
        step = solve(full, jnp.exp(theta), theta, theta_ref[...])
        out_ref[0:K] = theta
        out_ref[K:] = step
        theta = theta + step
        theta_now[...] = theta
        wait_reply(reply_out, reply_send)

        @pl.when(it < ITERS - 1)
        def _():
            spread_amp(theta)
            reply()

        return carry

    lax.fori_loop(0, ITERS, sweep, 0)
    wait_rows(rows_out, rows_send)


def local(
    stamps,
    stamp_gain,
    stamp_invvar,
    stamp_dest,
    stamp_obj,
    phi_tpl,
    psi_tpl,
    theta_init,
    nb_id,
    nb_weight,
):
    n_dev = lax.axis_size("sky")
    n_stamp, n_band, pix = stamps.shape
    n_obj = theta_init.shape[1]
    chunk = pix
    n_chunk = n_band * (pix // chunk)
    table = jnp.asarray(expand_table(), BF16)
    n_slot = n_dev * CAP
    operands = (
        jnp.transpose(stamps, (1, 0, 2)),
        stamp_gain,
        stamp_invvar,
        stamp_dest.reshape(1, n_stamp),
        stamp_obj.reshape(1, n_stamp),
        phi_tpl,
        psi_tpl,
        theta_init,
        nb_id.T,
        nb_weight.T,
        table,
    )
    scratch = [pltpu.VMEM(a.shape, a.dtype) for a in operands[1:]] + [
        pltpu.VMEM((8, 128), F32),
        pltpu.VMEM((n_chunk, n_stamp, chunk), BF16),
        pltpu.VMEM((n_chunk, 256, chunk), BF16),
        pltpu.VMEM((n_chunk, 32, chunk), BF16),
        pltpu.VMEM((n_stamp, 256), F32),
        pltpu.VMEM((K, n_stamp), F32),
        pltpu.VMEM((n_slot, n_stamp), BF16),
        pltpu.VMEM((n_dev, n_stamp), BF16),
        pltpu.VMEM((n_stamp, n_dev), BF16),
        pltpu.VMEM((n_stamp, 3 * n_dev), BF16),
        pltpu.VMEM((n_stamp, 128), F32),
        pltpu.VMEM((128, n_stamp), F32),
        pltpu.VMEM((n_stamp, 128), F32),
        pltpu.VMEM((n_stamp, 128), F32),
        pltpu.VMEM((n_obj, n_slot), BF16),
        pltpu.VMEM((n_obj, n_slot), BF16),
        pltpu.VMEM((4 * n_dev, CAP * n_obj), BF16),
        pltpu.VMEM((2, 3 * n_dev, CAP * n_obj), BF16),
        pltpu.VMEM((CAP * K, CAP * n_obj), BF16),
        pltpu.VMEM((CAP * n_dev, 5 * 128), BF16),
        pltpu.VMEM((3, CAP * K, CAP * n_obj), BF16),
        pltpu.VMEM((K, n_obj), F32),
        pltpu.VMEM((n_dev + 8, 128), F32),
        pltpu.VMEM((3, n_dev, 128), F32),
        pltpu.VMEM((2, 8, 128), F32),
        pltpu.VMEM((n_dev, CAP + 2, 128), F32),
        pltpu.VMEM((n_dev, CAP + 2, 128), F32),
        pltpu.VMEM((4, n_dev, 128), F32),
        pltpu.VMEM((4, n_dev, 128), F32),
        pltpu.VMEM((ITERS, n_obj, 384), F32),
        pltpu.VMEM((ITERS, n_obj, 384), F32),
        pltpu.SemaphoreType.DMA((10,)),
        pltpu.SemaphoreType.DMA((n_chunk,)),
        pltpu.SemaphoreType.DMA,
        pltpu.SemaphoreType.DMA,
        pltpu.SemaphoreType.DMA((2,)),
        pltpu.SemaphoreType.DMA((2,)),
        pltpu.SemaphoreType.DMA,
        pltpu.SemaphoreType.DMA,
        pltpu.SemaphoreType.DMA,
        pltpu.SemaphoreType.DMA,
        pltpu.SemaphoreType.DMA((ITERS,)),
        pltpu.SemaphoreType.DMA((ITERS,)),
    ]
    fitted = pl.pallas_call(
        functools.partial(kernel, (n_dev, n_stamp, n_obj, pix, chunk)),
        out_shape=jax.ShapeDtypeStruct((2 * K, n_obj), F32),
        in_specs=[pl.BlockSpec(memory_space=pltpu.HBM)] * len(operands),
        out_specs=pl.BlockSpec(memory_space=pltpu.VMEM),
        scratch_shapes=scratch,
        compiler_params=pltpu.CompilerParams(
            collective_id=0, has_side_effects=True, vmem_limit_bytes=(64 << 20) - (1 << 16)
        ),
    )(*operands)
    return fitted[:K] + fitted[K:]


def solution(mesh):
    in_specs = (
        P("sky", "band", None),
        P("sky"),
        P("sky"),
        P("sky", None),
        P("sky"),
        P("band", None, None),
        P("band", None, None),
        P(None, "sky"),
        P("sky", None),
        P("sky", None),
    )
    out_specs = P(None, "sky")
    return jax.shard_map(local, mesh=mesh, in_specs=in_specs, out_specs=out_specs, check_vma=False)
```

```python
import functools

import jax
import jax.numpy as jnp
import numpy as np
from jax import lax
from jax.experimental import pallas as pl
from jax.experimental.pallas import tpu as pltpu
from jax.sharding import PartitionSpec as P

ITERS = 3
CAP = 8
K = 16
ROBUST = 9.0
DAMPING = 0.1
PRIOR = 1.0
STEP_LIMIT = 0.5

MESH = pl.DeviceIdType.MESH
F32 = jnp.float32
BF16 = jnp.bfloat16


def iota(shape, dim):
    return lax.broadcasted_iota(jnp.int32, shape, dim)


def split(x):
    high = x.astype(BF16)
    return high, (x - high.astype(F32)).astype(BF16)


def split3(x):
    high, rest = x.astype(BF16), x - x.astype(BF16).astype(F32)
    middle = rest.astype(BF16)
    return high, middle, (rest - middle.astype(F32)).astype(BF16)


def dot(a, b):
    return jnp.dot(a, b, preferred_element_type=F32)


def dot_t(a, b):
    return lax.dot_general(a, b, (((1,), (1,)), ((), ())), preferred_element_type=F32)


def dot_exact(a, x):
    width = x.shape[1]
    sums = dot(a, jnp.concatenate(split3(x), axis=1))
    return sums[:, :width] + (sums[:, width : 2 * width] + sums[:, 2 * width :])


def dot_close(a, x):
    width = x.shape[1]
    sums = dot(a, jnp.concatenate(split(x), axis=1))
    return sums[:, :width] + sums[:, width:]


def dot_t_exact(a, x):
    high, middle, low = split3(x)
    return dot_t(a, high) + (dot_t(a, middle) + dot_t(a, low))


def expand_table():
    table = np.zeros((K * K + K, 384), np.float32)
    for k in range(K):
        for l in range(K):
            a, b = min(k, l), max(k, l)
            if a < 8:
                table[k * K + l, a * K + b] = 1
            elif a == b:
                table[k * K + l, 256 + np.arange(CAP) * K + a - 8] = 1
            else:
                table[k * K + l, (b - 8) * K + a - 8] = 1
        table[K * K + k, 128 + np.arange(CAP) * K + k] = 1
    return table


def offsets(side):
    steps = [(x, y, z) for x in range(side) for y in range(side) for z in range(side)]
    return sorted(steps[1:], key=lambda s: -sum(min(d, side - d) for d in s))


def solve(full, amp, theta, theta_init):
    sub8 = iota((8, amp.shape[1]), 0)
    amp_lo, amp_hi = amp[:8], amp[8:]
    first, second = [], []
    for k in range(K):
        own = amp[k : k + 1]
        row = full[k * K : k * K + K]
        if k < 8:
            part = row[:8] * (amp_lo * own)
            first.append(part + jnp.where(sub8 == k, DAMPING * part + PRIOR, 0.0))
        else:
            first.append(None)
        part = row[8:] * (amp_hi * own)
        if k >= 8:
            part = part + jnp.where(sub8 == k - 8, DAMPING * part + PRIOR, 0.0)
        second.append(part)
    target = full[K * K :] * amp - PRIOR * (theta - theta_init)
    t0, t1 = target[:8], target[8:]
    ups0, ups1, solved = [], [], []
    for p in range(K):
        r0, r1 = first[p], second[p]
        pivot = r0[p : p + 1] if p < 8 else r1[p - 8 : p - 7]
        inv = 1.0 / pivot
        s0 = None if r0 is None else r0 * inv
        s1 = r1 * inv
        y = (t0[p : p + 1] if p < 8 else t1[p - 8 : p - 7]) * inv
        ups0.append(None if s0 is None else jnp.where(sub8 > p, s0, 0.0))
        ups1.append(jnp.where(sub8 > p - 8, s1, 0.0))
        solved.append(y)
        if r0 is not None:
            t0 = t0 - r0 * y
        t1 = t1 - r1 * y
        for k in range(p + 1, K):
            factor = s0[k : k + 1] if k < 8 else s1[k - 8 : k - 7]
            if k < 8:
                first[k] = first[k] - factor * r0
            second[k] = second[k] - factor * r1
    x0 = jnp.zeros_like(t0)
    x1 = jnp.zeros_like(t1)
    for p in reversed(range(K)):
        known = ups1[p] * x1
        if p < 8:
            known = known + ups0[p] * x0
        value = solved[p] - jnp.sum(known, axis=0, keepdims=True)
        if p < 8:
            x0 = jnp.where(sub8 == p, value, x0)
        else:
            x1 = jnp.where(sub8 == p - 8, value, x1)
    delta = jnp.concatenate([x0, x1], axis=0)
    return STEP_LIMIT * jnp.tanh(delta / STEP_LIMIT)


def kernel(
    dims,
    stamps_ref,
    gain_hbm,
    invvar_hbm,
    dest_hbm,
    obj_hbm,
    phi_hbm,
    psi_hbm,
    theta_hbm,
    nb_id_hbm,
    nb_weight_hbm,
    table_hbm,
    out_ref,
    gain_ref,
    invvar_ref,
    dest_ref,
    obj_ref,
    phi_ref,
    psi_ref,
    theta_ref,
    nb_id_ref,
    nb_weight_ref,
    table_ref,
    nb_ref,
    pixels,
    pair,
    both,
    gram,
    proj,
    to_slot,
    to_dest,
    from_lit,
    from_near,
    gain_mask,
    gain_rows,
    plain_mask,
    stamp_cols,
    member,
    member2,
    reply_hi,
    reply_lo,
    reply_mask,
    rest_mask,
    amp_parts,
    theta_now,
    meta_out,
    meta_in,
    nb_in,
    rows_out,
    rows_in,
    reply_out,
    reply_in,
    sums_out,
    sums_in,
    in_sem,
    pix_sem,
    meta_send,
    meta_recv,
    nb_send,
    nb_recv,
    rows_send,
    rows_recv,
    reply_send,
    reply_recv,
    sums_send,
    sums_recv,
):
    n_dev, n_stamp, n_obj, pix, chunk = dims
    per_band = pix // chunk
    n_chunk = pixels.shape[0]
    n_slot = n_dev * CAP
    me = lax.axis_index("sky")
    core = lax.axis_index("band")

    def peer(j):
        return lax.rem(me + j, n_dev)

    side = 4
    x, y, z = me // (side * side), lax.rem(me // side, side), lax.rem(me, side)
    along_x = [lax.rem(x + d, side) * (side * side) for d in range(side)]
    along_y = [lax.rem(y + d, side) * side for d in range(side)]
    along_z = [lax.rem(z + d, side) for d in range(side)]

    def each_peer(act):
        if n_dev == side**3:
            for dx, dy, dz in offsets(side):
                act(along_x[dx] + along_y[dy] + along_z[dz])
        else:

            def step(j, carry):
                act(peer(j))
                return carry

            lax.fori_loop(1, n_dev, step, 0)

    barrier = pltpu.get_barrier_semaphore()

    def greet(t):
        pl.semaphore_signal(barrier, inc=1, device_id=(t, core), device_id_type=MESH)

    each_peer(greet)
    pl.semaphore_signal(barrier, inc=1, device_id=(me, 1 - core), device_id_type=MESH)

    in_copies = []
    for i, (src, dst) in enumerate(
        (
            (gain_hbm, gain_ref),
            (invvar_hbm, invvar_ref),
            (dest_hbm, dest_ref),
            (obj_hbm, obj_ref),
            (nb_id_hbm, nb_id_ref),
            (nb_weight_hbm, nb_weight_ref),
            (theta_hbm, theta_ref),
            (table_hbm, table_ref),
            (phi_hbm, phi_ref),
            (psi_hbm, psi_ref),
        )
    ):
        copy = pltpu.make_async_copy(src, dst, in_sem.at[i])
        copy.start()
        in_copies.append(copy)
    pixel_copies = []
    for i in range(n_chunk):
        band, part = divmod(i, per_band)
        copy = pltpu.make_async_copy(
            stamps_ref.at[band, :, pl.ds(part * chunk, chunk)], pixels.at[i], pix_sem.at[i]
        )
        copy.start()
        pixel_copies.append(copy)

    for copy in in_copies[:8]:
        copy.wait()
    small = jnp.concatenate(
        [
            gain_ref[...].astype(F32).reshape(1, n_stamp),
            invvar_ref[...].astype(F32).reshape(1, n_stamp),
            dest_ref[...].astype(F32).reshape(1, n_stamp),
            obj_ref[...].astype(F32).reshape(1, n_stamp),
            jnp.zeros((4, n_stamp), F32),
        ],
        axis=0,
    )
    nb_ref[...] = jnp.zeros_like(nb_ref)
    nb_ref[0:4, 0:n_obj] = nb_id_ref[...].astype(F32)
    nb_ref[4:8, 0:n_obj] = nb_weight_ref[...]
    cols = jnp.concatenate([small, jnp.zeros((120, n_stamp), F32)], axis=0).T
    gain_row, dest_row, obj_row = small[0:1], small[2:3], small[3:4]
    gain_col, invvar_col, dest_col = cols[:, 0:1], cols[:, 1:2], cols[:, 2:3]
    same = dest_col == dest_row
    low = iota((n_stamp, n_stamp), 0)
    across = iota((n_stamp, n_stamp), 1)
    rank_col = jnp.sum(jnp.where(same & (across < low), 1.0, 0.0), axis=1, keepdims=True)
    rank_row = jnp.sum(jnp.where(same & (low < across), 1.0, 0.0), axis=0, keepdims=True)
    dest_hot = jnp.where(iota((n_dev, n_stamp), 0).astype(F32) == dest_row, 1.0, 0.0).astype(BF16)
    to_dest[...] = dest_hot
    obj_col = cols[:, 3:4]
    named = jnp.where(iota((n_stamp, 128), 1).astype(F32) == rank_col, obj_col + 1.0, 0.0)
    slot_obj = dot(dest_hot, named.astype(BF16))
    meta_out[1 : n_dev + 1] = slot_obj
    meta_out[0:1] = slot_obj[n_dev - 1 :]
    meta_out[n_dev + 1 : n_dev + 2] = slot_obj[:1]

    pl.semaphore_wait(barrier, n_dev)

    nb_copies = []
    for side, step in ((0, 1), (1, n_dev - 1)):
        copy = pltpu.make_async_remote_copy(
            nb_ref,
            nb_in.at[side],
            nb_send.at[side],
            nb_recv.at[side],
            device_id=(peer(step), core),
            device_id_type=MESH,
        )
        copy.start()
        nb_copies.append(copy)
    def send_meta(t):
        pltpu.make_async_remote_copy(
            meta_out.at[pl.ds(t, 3)],
            meta_in.at[:, me],
            meta_send,
            meta_recv,
            device_id=(t, core),
            device_id_type=MESH,
        ).start()

    each_peer(send_meta)
    for r in range(3):
        meta_in[r, pl.ds(me, 1), :] = meta_out[pl.ds(me + r, 1), :]

    slot_row = dest_row * CAP + rank_row
    to_slot[...] = jnp.where(iota((n_slot, n_stamp), 0).astype(F32) == slot_row, 1.0, 0.0).astype(BF16)
    dest_int = dest_col.astype(jnp.int32)
    owner = iota((n_stamp, n_dev), 1)
    from_lit[...] = jnp.where(owner == dest_int, 1.0, 0.0).astype(BF16)
    shifted = []
    for r in range(3):
        want = dest_int + 1 - r
        want = jnp.where(want < 0, want + n_dev, jnp.where(want >= n_dev, want - n_dev, want))
        shifted.append(jnp.where(owner == want, 1.0, 0.0))
    from_near[...] = jnp.concatenate(shifted, axis=1).astype(BF16)
    group = (iota((n_stamp, 128), 1) // K).astype(F32)
    in_slot = jnp.where(group == rank_col, 1.0, 0.0)
    plain_mask[...] = in_slot
    gain_mask[...] = in_slot * gain_col
    in_slot_row = (iota((128, n_stamp), 0) // K).astype(F32) == rank_row
    gain_rows[...] = jnp.where(in_slot_row, gain_row, 0.0)
    lane = iota((n_stamp, 128), 1)
    stamp_cols[...] = jnp.where(lane == 0, gain_col, jnp.where(lane == 1, ROBUST / invvar_col, 0.0))

    def build(i, carry):
        band = i // per_band
        at = pl.multiple_of((i % per_band) * chunk, chunk)
        phi16 = phi_ref[band, :, pl.ds(at, chunk)]
        phi = phi16.astype(F32)
        swapped = jnp.concatenate([phi[8:], phi[:8]], axis=0)
        sub = iota((K, chunk), 0)
        for k in range(8):
            block = jnp.where(sub >= k, phi * phi[k : k + 1], swapped * phi[8 + k : 9 + k])
            pair[i, k * K : (k + 1) * K, :] = block.astype(BF16)
        rest = (swapped * swapped).astype(BF16)
        for c in range(CAP):
            pair[i, 128 + c * K : 128 + (c + 1) * K, :] = rest
        both[i, 0:K, :] = phi16
        both[i, K : 2 * K, :] = psi_ref[band, :, pl.ds(at, chunk)]
        return carry

    pairs = CAP // 2
    shape = (CAP * K, CAP * n_obj)
    reply_mask[...] = jnp.where(iota(shape, 0) // K == iota(shape, 1) // n_obj, 1.0, 0.0).astype(BF16)

    def spread_amp(theta):
        for part, amp in enumerate(split3(jnp.exp(theta))):
            double = jnp.concatenate([amp, amp], axis=1)
            tiled = jnp.concatenate([double] * pairs, axis=1)
            amp_parts[part] = jnp.concatenate([tiled] * CAP, axis=0) * reply_mask[...]

    spread_amp(theta_ref[...])
    wanted = (iota((n_obj, n_obj), 0) + me * n_obj).astype(F32)

    def blend_of(table):
        blend = jnp.zeros((n_obj, n_obj), F32)
        for j in range(4):
            blend = blend + jnp.where(wanted == table[j : j + 1, :n_obj], table[4 + j : 5 + j, :n_obj], 0.0)
        zero = jnp.zeros_like(blend)
        twice = jnp.concatenate(
            [jnp.concatenate([blend, zero], axis=1), jnp.concatenate([zero, blend], axis=1)], axis=0
        )
        return jnp.concatenate(split(twice), axis=0)

    blends = [None, blend_of(nb_ref[...]), None]
    for copy in nb_copies:
        copy.wait()
    blends[0], blends[2] = blend_of(nb_in[0]), blend_of(nb_in[1])
    meta_part = meta_in.at[:, pl.ds(0, n_dev - 1)]
    pltpu.make_async_copy(meta_part, meta_part, meta_recv).wait()
    lane = iota((n_dev, 2 * n_obj), 1)
    number = (lane % n_obj).astype(F32) + 1.0
    for r in range(3):
        objects = meta_in[r]
        hots = [
            jnp.where(
                jnp.where(lane < n_obj, objects[:, 2 * i : 2 * i + 1], objects[:, 2 * i + 1 : 2 * i + 2]) == number,
                1.0,
                0.0,
            ).astype(BF16)
            for i in range(pairs)
        ]
        if r == 1:
            reply_hi[0:n_dev, :] = jnp.concatenate(hots, axis=1)
        weights = dot_t(jnp.concatenate(hots, axis=0), blends[r]).astype(BF16)
        at = (1 + r) * n_dev
        for i in range(pairs):
            own = weights[i * n_dev : (i + 1) * n_dev]
            columns = slice(i * 2 * n_obj, (i + 1) * 2 * n_obj)
            reply_hi[at : at + n_dev, columns] = own[:, : 2 * n_obj]
            reply_lo[at - n_dev : at, columns] = own[:, 2 * n_obj :]

    def reply():
        for part in range(3):
            term = dot_t(reply_hi[0:n_dev, :], amp_parts[part])
            lit = term if part == 0 else lit + term
        reply_out[0] = lit
        near = dot_t(reply_hi[n_dev:, :], amp_parts[1]) + dot_t(reply_lo[...], amp_parts[0])
        near = near + dot_t(reply_hi[n_dev:, :], amp_parts[0])
        for r in range(3):
            reply_out[1 + r] = near[r * n_dev : (r + 1) * n_dev]

        def send(t):
            pltpu.make_async_remote_copy(
                reply_out.at[:, pl.ds(t, 1)],
                reply_in.at[:, pl.ds(me, 1)],
                reply_send,
                reply_recv,
                device_id=(t, core),
                device_id_type=MESH,
            ).start()

        each_peer(send)
        reply_in[:, pl.ds(me, 1), :] = reply_out[:, pl.ds(me, 1), :]

    def wait_reply(ref, sem):
        part = ref.at[:, pl.ds(0, n_dev - 1)]
        pltpu.make_async_copy(part, part, sem).wait()

    def wait_rows(ref, sem):
        part = ref.at[pl.ds(0, n_dev - 1)]
        pltpu.make_async_copy(part, part, sem).wait()

    theta_now[...] = theta_ref[...]
    reply()
    shape = (CAP * n_dev, 5 * 128)
    rest_mask[...] = jnp.where(
        iota(shape, 0) // n_dev == (iota(shape, 1) % 128) // K, 1.0, 0.0
    ).astype(BF16)
    own_obj = meta_in[1]
    turned = dot_t(
        jnp.where(iota((128, 128), 0) == iota((128, 128), 1), 1.0, 0.0).astype(BF16), own_obj.astype(BF16)
    )
    placed = dot(
        turned.astype(BF16),
        jnp.where(iota((n_dev, n_slot), 1) // CAP == iota((n_dev, n_slot), 0), 1.0, 0.0).astype(BF16),
    )[:CAP]
    mine = iota((CAP, n_slot), 1) % CAP == iota((CAP, n_slot), 0)
    obj_of_slot = jnp.sum(jnp.where(mine, placed, 0.0), axis=0, keepdims=True)
    member[...] = jnp.where(
        iota((n_obj, n_slot), 0).astype(F32) + 1.0 == obj_of_slot, 1.0, 0.0
    ).astype(BF16)
    obj_sub = iota((n_obj, n_dev), 0).astype(F32) + 1.0
    member2[...] = jnp.concatenate(
        [jnp.where(obj_sub == turned[c : c + 1], 1.0, 0.0) for c in range(CAP)], axis=1
    ).astype(BF16)
    for copy in in_copies[8:]:
        copy.wait()
    lax.fori_loop(0, n_chunk, build, 0)
    pltpu.make_async_copy(meta_part, meta_part, meta_send).wait()
    for copy in pixel_copies:
        copy.wait()

    fold_shape = (2 * CAP * K, 2 * K)
    fold_row, fold_col = iota(fold_shape, 0), iota(fold_shape, 1)
    fold = jnp.where(
        (fold_row // (CAP * K) == fold_col // K) & (fold_row % K == fold_col % K), 1.0, 0.0
    ).astype(BF16)

    def sweep(it, carry):
        wait_reply(reply_in, reply_recv)
        near = jnp.concatenate([reply_in[r] for r in (1, 2, 3)], axis=0)
        lit = dot_exact(from_lit[...], reply_in[0])
        near = dot_close(from_near[...], near)
        wide = jnp.concatenate([lit * gain_mask[...], near * plain_mask[...]], axis=1)
        coeff = dot(wide.astype(BF16), fold).astype(BF16)
        gain = stamp_cols[:, 0:1]
        softening = stamp_cols[:, 1:2]
        gram[...] = jnp.zeros_like(gram)
        proj[...] = jnp.zeros_like(proj)

        def one_chunk(i):
            resid = pixels[i].astype(F32) - dot(coeff, both[i])
            weight = ROBUST / (resid * resid + softening)
            gram[...] += dot_t(weight.astype(BF16), pair[i])
            proj[...] += dot_t(both[i, 0:K, :], (weight * resid).astype(BF16))

        for i in range(n_chunk):
            one_chunk(i)
        main = dot_close(to_slot[...], gram[:, :128] * (gain * gain))
        rest_proj = dot_t_exact(to_dest[...], jnp.concatenate([proj[...]] * CAP, axis=0) * gain_rows[...])
        rest_diag = dot_close(to_dest[...], gram[:, 128:] * (gain_mask[...] * gain))

        @pl.when(it > 0)
        def _():
            wait_rows(rows_out, rows_send)

        rows_out[:, 0:CAP, :] = main.reshape(n_dev, CAP, 128)
        rows_out[:, CAP, :] = rest_proj
        rows_out[:, CAP + 1, :] = rest_diag

        def send(t):
            pltpu.make_async_remote_copy(
                rows_out.at[t],
                rows_in.at[me],
                rows_send,
                rows_recv,
                device_id=(t, core),
                device_id_type=MESH,
            ).start()

        each_peer(send)
        rows_in[me] = rows_out[me]

        wait_rows(rows_in, rows_recv)
        main_sum = dot_close(member[...], rows_in[:, 0:CAP, :].reshape(n_slot, 128))
        parts = split3(rows_in[:, CAP, :]) + split(rows_in[:, CAP + 1, :])
        parts = jnp.concatenate(parts, axis=1)
        parts = dot(member2[...], jnp.concatenate([parts] * CAP, axis=0) * rest_mask[...])
        proj_sum = parts[:, 0:128] + (parts[:, 128:256] + parts[:, 256:384])
        rest_sum = jnp.concatenate([proj_sum, parts[:, 384:512] + parts[:, 512:640]], axis=1)
        sums = jnp.concatenate([main_sum, rest_sum], axis=1)
        sums_out[it] = sums
        copy = pltpu.make_async_remote_copy(
            sums_out.at[it],
            sums_in.at[it],
            sums_send.at[it],
            sums_recv.at[it],
            device_id=(me, 1 - core),
            device_id_type=MESH,
        )
        copy.start()
        copy.wait()
        full = dot_t_exact(table_ref[...], sums + sums_in[it])
        theta = theta_now[...]
        step = solve(full, jnp.exp(theta), theta, theta_ref[...])
        out_ref[0:K] = theta
        out_ref[K:] = step
        theta = theta + step
        theta_now[...] = theta
        wait_reply(reply_out, reply_send)

        @pl.when(it < ITERS - 1)
        def _():
            spread_amp(theta)
            reply()

        return carry

    lax.fori_loop(0, ITERS, sweep, 0)
    wait_rows(rows_out, rows_send)


def local(
    stamps,
    stamp_gain,
    stamp_invvar,
    stamp_dest,
    stamp_obj,
    phi_tpl,
    psi_tpl,
    theta_init,
    nb_id,
    nb_weight,
):
    n_dev = lax.axis_size("sky")
    n_stamp, n_band, pix = stamps.shape
    n_obj = theta_init.shape[1]
    chunk = pix
    n_chunk = n_band * (pix // chunk)
    table = jnp.asarray(expand_table(), BF16)
    n_slot = n_dev * CAP
    operands = (
        jnp.transpose(stamps, (1, 0, 2)),
        stamp_gain,
        stamp_invvar,
        stamp_dest.reshape(1, n_stamp),
        stamp_obj.reshape(1, n_stamp),
        phi_tpl,
        psi_tpl,
        theta_init,
        nb_id.T,
        nb_weight.T,
        table,
    )
    scratch = [pltpu.VMEM(a.shape, a.dtype) for a in operands[1:]] + [
        pltpu.VMEM((8, 128), F32),
        pltpu.VMEM((n_chunk, n_stamp, chunk), BF16),
        pltpu.VMEM((n_chunk, 256, chunk), BF16),
        pltpu.VMEM((n_chunk, 32, chunk), BF16),
        pltpu.VMEM((n_stamp, 256), F32),
        pltpu.VMEM((K, n_stamp), F32),
        pltpu.VMEM((n_slot, n_stamp), BF16),
        pltpu.VMEM((n_dev, n_stamp), BF16),
        pltpu.VMEM((n_stamp, n_dev), BF16),
        pltpu.VMEM((n_stamp, 3 * n_dev), BF16),
        pltpu.VMEM((n_stamp, 128), F32),
        pltpu.VMEM((128, n_stamp), F32),
        pltpu.VMEM((n_stamp, 128), F32),
        pltpu.VMEM((n_stamp, 128), F32),
        pltpu.VMEM((n_obj, n_slot), BF16),
        pltpu.VMEM((n_obj, n_slot), BF16),
        pltpu.VMEM((4 * n_dev, CAP * n_obj), BF16),
        pltpu.VMEM((3 * n_dev, CAP * n_obj), BF16),
        pltpu.VMEM((CAP * K, CAP * n_obj), BF16),
        pltpu.VMEM((CAP * n_dev, 5 * 128), BF16),
        pltpu.VMEM((3, CAP * K, CAP * n_obj), BF16),
        pltpu.VMEM((K, n_obj), F32),
        pltpu.VMEM((n_dev + 8, 128), F32),
        pltpu.VMEM((3, n_dev, 128), F32),
        pltpu.VMEM((2, 8, 128), F32),
        pltpu.VMEM((n_dev, CAP + 2, 128), F32),
        pltpu.VMEM((n_dev, CAP + 2, 128), F32),
        pltpu.VMEM((4, n_dev, 128), F32),
        pltpu.VMEM((4, n_dev, 128), F32),
        pltpu.VMEM((ITERS, n_obj, 384), F32),
        pltpu.VMEM((ITERS, n_obj, 384), F32),
        pltpu.SemaphoreType.DMA((10,)),
        pltpu.SemaphoreType.DMA((n_chunk,)),
        pltpu.SemaphoreType.DMA,
        pltpu.SemaphoreType.DMA,
        pltpu.SemaphoreType.DMA((2,)),
        pltpu.SemaphoreType.DMA((2,)),
        pltpu.SemaphoreType.DMA,
        pltpu.SemaphoreType.DMA,
        pltpu.SemaphoreType.DMA,
        pltpu.SemaphoreType.DMA,
        pltpu.SemaphoreType.DMA((ITERS,)),
        pltpu.SemaphoreType.DMA((ITERS,)),
    ]
    fitted = pl.pallas_call(
        functools.partial(kernel, (n_dev, n_stamp, n_obj, pix, chunk)),
        out_shape=jax.ShapeDtypeStruct((2 * K, n_obj), F32),
        in_specs=[pl.BlockSpec(memory_space=pltpu.HBM)] * len(operands),
        out_specs=pl.BlockSpec(memory_space=pltpu.VMEM),
        scratch_shapes=scratch,
        compiler_params=pltpu.CompilerParams(
            collective_id=0, has_side_effects=True, vmem_limit_bytes=(64 << 20) - (1 << 16)
        ),
    )(*operands)
    return fitted[:K] + fitted[K:]


def solution(mesh):
    in_specs = (
        P("sky", "band", None),
        P("sky"),
        P("sky"),
        P("sky", None),
        P("sky"),
        P("band", None, None),
        P("band", None, None),
        P(None, "sky"),
        P("sky", None),
        P("sky", None),
    )
    out_specs = P(None, "sky")
    return jax.shard_map(local, mesh=mesh, in_specs=in_specs, out_specs=out_specs, check_vma=False)
```

```python
import functools

import jax
import jax.numpy as jnp
import numpy as np
from jax import lax
from jax.experimental import pallas as pl
from jax.experimental.pallas import tpu as pltpu
from jax.sharding import PartitionSpec as P

ITERS = 3
CAP = 8
K = 16
ROBUST = 9.0
DAMPING = 0.1
PRIOR = 1.0
STEP_LIMIT = 0.5

MESH = pl.DeviceIdType.MESH
F32 = jnp.float32
BF16 = jnp.bfloat16


def iota(shape, dim):
    return lax.broadcasted_iota(jnp.int32, shape, dim)


def split(x):
    high = x.astype(BF16)
    return high, (x - high.astype(F32)).astype(BF16)


def split3(x):
    high, rest = x.astype(BF16), x - x.astype(BF16).astype(F32)
    middle = rest.astype(BF16)
    return high, middle, (rest - middle.astype(F32)).astype(BF16)


def dot(a, b):
    return jnp.dot(a, b, preferred_element_type=F32)


def dot_t(a, b):
    return lax.dot_general(a, b, (((1,), (1,)), ((), ())), preferred_element_type=F32)


def dot_exact(a, x):
    width = x.shape[1]
    sums = dot(a, jnp.concatenate(split3(x), axis=1))
    return sums[:, :width] + (sums[:, width : 2 * width] + sums[:, 2 * width :])


def dot_close(a, x):
    width = x.shape[1]
    sums = dot(a, jnp.concatenate(split(x), axis=1))
    return sums[:, :width] + sums[:, width:]


def dot_t_exact(a, x):
    high, middle, low = split3(x)
    return dot_t(a, high) + (dot_t(a, middle) + dot_t(a, low))


def expand_table():
    table = np.zeros((K * K + K, 384), np.float32)
    for k in range(K):
        for l in range(K):
            a, b = min(k, l), max(k, l)
            if a < 8:
                table[k * K + l, a * K + b] = 1
            elif a == b:
                table[k * K + l, 256 + np.arange(CAP) * K + a - 8] = 1
            else:
                table[k * K + l, (b - 8) * K + a - 8] = 1
        table[K * K + k, 128 + np.arange(CAP) * K + k] = 1
    return table


def offsets(side):
    steps = [(x, y, z) for x in range(side) for y in range(side) for z in range(side)]
    return sorted(steps[1:], key=lambda s: -sum(min(d, side - d) for d in s))


def solve(full, amp, theta, theta_init):
    sub8 = iota((8, amp.shape[1]), 0)
    amp_lo, amp_hi = amp[:8], amp[8:]
    first, second = [], []
    for k in range(K):
        own = amp[k : k + 1]
        row = full[k * K : k * K + K]
        if k < 8:
            part = row[:8] * (amp_lo * own)
            first.append(part + jnp.where(sub8 == k, DAMPING * part + PRIOR, 0.0))
        else:
            first.append(None)
        part = row[8:] * (amp_hi * own)
        if k >= 8:
            part = part + jnp.where(sub8 == k - 8, DAMPING * part + PRIOR, 0.0)
        second.append(part)
    target = full[K * K :] * amp - PRIOR * (theta - theta_init)
    t0, t1 = target[:8], target[8:]
    ups0, ups1, solved = [], [], []
    for p in range(K):
        r0, r1 = first[p], second[p]
        pivot = r0[p : p + 1] if p < 8 else r1[p - 8 : p - 7]
        inv = 1.0 / pivot
        s0 = None if r0 is None else r0 * inv
        s1 = r1 * inv
        y = (t0[p : p + 1] if p < 8 else t1[p - 8 : p - 7]) * inv
        ups0.append(None if s0 is None else jnp.where(sub8 > p, s0, 0.0))
        ups1.append(jnp.where(sub8 > p - 8, s1, 0.0))
        solved.append(y)
        if r0 is not None:
            t0 = t0 - r0 * y
        t1 = t1 - r1 * y
        for k in range(p + 1, K):
            factor = s0[k : k + 1] if k < 8 else s1[k - 8 : k - 7]
            if k < 8:
                first[k] = first[k] - factor * r0
            second[k] = second[k] - factor * r1
    x0 = jnp.zeros_like(t0)
    x1 = jnp.zeros_like(t1)
    for p in reversed(range(K)):
        known = ups1[p] * x1
        if p < 8:
            known = known + ups0[p] * x0
        value = solved[p] - jnp.sum(known, axis=0, keepdims=True)
        if p < 8:
            x0 = jnp.where(sub8 == p, value, x0)
        else:
            x1 = jnp.where(sub8 == p - 8, value, x1)
    delta = jnp.concatenate([x0, x1], axis=0)
    return STEP_LIMIT * jnp.tanh(delta / STEP_LIMIT)


def kernel(
    dims,
    stamps_ref,
    gain_hbm,
    invvar_hbm,
    dest_hbm,
    obj_hbm,
    phi_hbm,
    psi_hbm,
    theta_hbm,
    nb_id_hbm,
    nb_weight_hbm,
    table_hbm,
    out_ref,
    gain_ref,
    invvar_ref,
    dest_ref,
    obj_ref,
    phi_ref,
    psi_ref,
    theta_ref,
    nb_id_ref,
    nb_weight_ref,
    table_ref,
    nb_ref,
    pixels,
    pair,
    both,
    gram,
    proj,
    to_slot,
    to_dest,
    from_lit,
    from_near,
    gain_mask,
    gain_rows,
    plain_mask,
    stamp_cols,
    member,
    member2,
    reply_hi,
    reply_lo,
    reply_mask,
    rest_mask,
    amp_parts,
    theta_now,
    meta_out,
    meta_in,
    nb_in,
    rows_out,
    rows_in,
    reply_out,
    reply_in,
    sums_out,
    sums_in,
    in_sem,
    pix_sem,
    meta_send,
    meta_recv,
    nb_send,
    nb_recv,
    rows_send,
    rows_recv,
    reply_send,
    reply_recv,
    sums_send,
    sums_recv,
):
    n_dev, n_stamp, n_obj, pix, chunk = dims
    per_band = pix // chunk
    n_chunk = pixels.shape[0]
    n_slot = n_dev * CAP
    me = lax.axis_index("sky")
    core = lax.axis_index("band")

    def peer(j):
        return lax.rem(me + j, n_dev)

    side = 4
    x, y, z = me // (side * side), lax.rem(me // side, side), lax.rem(me, side)
    along_x = [lax.rem(x + d, side) * (side * side) for d in range(side)]
    along_y = [lax.rem(y + d, side) * side for d in range(side)]
    along_z = [lax.rem(z + d, side) for d in range(side)]

    def each_peer(act):
        if n_dev == side**3:
            for dx, dy, dz in offsets(side):
                act(along_x[dx] + along_y[dy] + along_z[dz])
        else:

            def step(j, carry):
                act(peer(j))
                return carry

            lax.fori_loop(1, n_dev, step, 0)

    in_copies = []
    for i, (src, dst) in enumerate(
        (
            (gain_hbm, gain_ref),
            (invvar_hbm, invvar_ref),
            (dest_hbm, dest_ref),
            (obj_hbm, obj_ref),
            (nb_id_hbm, nb_id_ref),
            (nb_weight_hbm, nb_weight_ref),
            (theta_hbm, theta_ref),
            (table_hbm, table_ref),
            (phi_hbm, phi_ref),
            (psi_hbm, psi_ref),
        )
    ):
        copy = pltpu.make_async_copy(src, dst, in_sem.at[i])
        copy.start()
        in_copies.append(copy)
    barrier = pltpu.get_barrier_semaphore()

    def greet(t):
        pl.semaphore_signal(barrier, inc=1, device_id=(t, core), device_id_type=MESH)

    each_peer(greet)
    pl.semaphore_signal(barrier, inc=1, device_id=(me, 1 - core), device_id_type=MESH)

    pixel_copies = []
    for i in range(n_chunk):
        band, part = divmod(i, per_band)
        copy = pltpu.make_async_copy(
            stamps_ref.at[band, :, pl.ds(part * chunk, chunk)], pixels.at[i], pix_sem.at[i]
        )
        copy.start()
        pixel_copies.append(copy)

    for copy in in_copies[:8]:
        copy.wait()
    small = jnp.concatenate(
        [
            gain_ref[...].astype(F32).reshape(1, n_stamp),
            invvar_ref[...].astype(F32).reshape(1, n_stamp),
            dest_ref[...].astype(F32).reshape(1, n_stamp),
            obj_ref[...].astype(F32).reshape(1, n_stamp),
            jnp.zeros((4, n_stamp), F32),
        ],
        axis=0,
    )
    nb_ref[...] = jnp.zeros_like(nb_ref)
    nb_ref[0:4, 0:n_obj] = nb_id_ref[...].astype(F32)
    nb_ref[4:8, 0:n_obj] = nb_weight_ref[...]
    cols = jnp.concatenate([small, jnp.zeros((120, n_stamp), F32)], axis=0).T
    gain_row, dest_row, obj_row = small[0:1], small[2:3], small[3:4]
    gain_col, invvar_col, dest_col = cols[:, 0:1], cols[:, 1:2], cols[:, 2:3]
    same = dest_col == dest_row
    low = iota((n_stamp, n_stamp), 0)
    across = iota((n_stamp, n_stamp), 1)
    rank_col = jnp.sum(jnp.where(same & (across < low), 1.0, 0.0), axis=1, keepdims=True)
    rank_row = jnp.sum(jnp.where(same & (low < across), 1.0, 0.0), axis=0, keepdims=True)
    dest_hot = jnp.where(iota((n_dev, n_stamp), 0).astype(F32) == dest_row, 1.0, 0.0).astype(BF16)
    to_dest[...] = dest_hot
    obj_col = cols[:, 3:4]
    named = jnp.where(iota((n_stamp, 128), 1).astype(F32) == rank_col, obj_col + 1.0, 0.0)
    slot_obj = dot(dest_hot, named.astype(BF16))
    meta_out[1 : n_dev + 1] = slot_obj
    meta_out[0:1] = slot_obj[n_dev - 1 :]
    meta_out[n_dev + 1 : n_dev + 2] = slot_obj[:1]

    pl.semaphore_wait(barrier, n_dev)

    nb_copies = []
    for side, step in ((0, 1), (1, n_dev - 1)):
        copy = pltpu.make_async_remote_copy(
            nb_ref,
            nb_in.at[side],
            nb_send.at[side],
            nb_recv.at[side],
            device_id=(peer(step), core),
            device_id_type=MESH,
        )
        copy.start()
        nb_copies.append(copy)
    def send_meta(t):
        pltpu.make_async_remote_copy(
            meta_out.at[pl.ds(t, 3)],
            meta_in.at[:, me],
            meta_send,
            meta_recv,
            device_id=(t, core),
            device_id_type=MESH,
        ).start()

    each_peer(send_meta)
    for r in range(3):
        meta_in[r, pl.ds(me, 1), :] = meta_out[pl.ds(me + r, 1), :]

    slot_row = dest_row * CAP + rank_row
    to_slot[...] = jnp.where(iota((n_slot, n_stamp), 0).astype(F32) == slot_row, 1.0, 0.0).astype(BF16)
    dest_int = dest_col.astype(jnp.int32)
    owner = iota((n_stamp, n_dev), 1)
    from_lit[...] = jnp.where(owner == dest_int, 1.0, 0.0).astype(BF16)
    shifted = []
    for r in range(3):
        want = dest_int + 1 - r
        want = jnp.where(want < 0, want + n_dev, jnp.where(want >= n_dev, want - n_dev, want))
        shifted.append(jnp.where(owner == want, 1.0, 0.0))
    from_near[...] = jnp.concatenate(shifted, axis=1).astype(BF16)
    group = (iota((n_stamp, 128), 1) // K).astype(F32)
    in_slot = jnp.where(group == rank_col, 1.0, 0.0)
    plain_mask[...] = in_slot
    gain_mask[...] = in_slot * gain_col
    in_slot_row = (iota((128, n_stamp), 0) // K).astype(F32) == rank_row
    gain_rows[...] = jnp.where(in_slot_row, gain_row, 0.0)
    lane = iota((n_stamp, 128), 1)
    stamp_cols[...] = jnp.where(lane == 0, gain_col, jnp.where(lane == 1, ROBUST / invvar_col, 0.0))

    def build(i, carry):
        band = i // per_band
        at = pl.multiple_of((i % per_band) * chunk, chunk)
        phi16 = phi_ref[band, :, pl.ds(at, chunk)]
        phi = phi16.astype(F32)
        swapped = jnp.concatenate([phi[8:], phi[:8]], axis=0)
        sub = iota((K, chunk), 0)
        for k in range(8):
            block = jnp.where(sub >= k, phi * phi[k : k + 1], swapped * phi[8 + k : 9 + k])
            pair[i, k * K : (k + 1) * K, :] = block.astype(BF16)
        rest = (swapped * swapped).astype(BF16)
        for c in range(CAP):
            pair[i, 128 + c * K : 128 + (c + 1) * K, :] = rest
        both[i, 0:K, :] = phi16
        both[i, K : 2 * K, :] = psi_ref[band, :, pl.ds(at, chunk)]
        return carry

    pairs = CAP // 2
    shape = (CAP * K, CAP * n_obj)
    reply_mask[...] = jnp.where(iota(shape, 0) // K == iota(shape, 1) // n_obj, 1.0, 0.0).astype(BF16)

    def spread_amp(theta):
        for part, amp in enumerate(split3(jnp.exp(theta))):
            double = jnp.concatenate([amp, amp], axis=1)
            tiled = jnp.concatenate([double] * pairs, axis=1)
            amp_parts[part] = jnp.concatenate([tiled] * CAP, axis=0) * reply_mask[...]

    spread_amp(theta_ref[...])
    wanted = (iota((n_obj, n_obj), 0) + me * n_obj).astype(F32)

    def blend_of(table):
        blend = jnp.zeros((n_obj, n_obj), F32)
        for j in range(4):
            blend = blend + jnp.where(wanted == table[j : j + 1, :n_obj], table[4 + j : 5 + j, :n_obj], 0.0)
        zero = jnp.zeros_like(blend)
        twice = jnp.concatenate(
            [jnp.concatenate([blend, zero], axis=1), jnp.concatenate([zero, blend], axis=1)], axis=0
        )
        return jnp.concatenate(split(twice), axis=0)

    blends = [None, blend_of(nb_ref[...]), None]
    for copy in nb_copies:
        copy.wait()
    blends[0], blends[2] = blend_of(nb_in[0]), blend_of(nb_in[1])
    meta_part = meta_in.at[:, pl.ds(0, n_dev - 1)]
    pltpu.make_async_copy(meta_part, meta_part, meta_recv).wait()
    lane = iota((n_dev, 2 * n_obj), 1)
    number = (lane % n_obj).astype(F32) + 1.0
    for r in range(3):
        objects = meta_in[r]
        hots = [
            jnp.where(
                jnp.where(lane < n_obj, objects[:, 2 * i : 2 * i + 1], objects[:, 2 * i + 1 : 2 * i + 2]) == number,
                1.0,
                0.0,
            ).astype(BF16)
            for i in range(pairs)
        ]
        if r == 1:
            reply_hi[0:n_dev, :] = jnp.concatenate(hots, axis=1)
        weights = dot_t(jnp.concatenate(hots, axis=0), blends[r]).astype(BF16)
        at = (1 + r) * n_dev
        for i in range(pairs):
            own = weights[i * n_dev : (i + 1) * n_dev]
            columns = slice(i * 2 * n_obj, (i + 1) * 2 * n_obj)
            reply_hi[at : at + n_dev, columns] = own[:, : 2 * n_obj]
            reply_lo[at - n_dev : at, columns] = own[:, 2 * n_obj :]

    def reply():
        for part in range(3):
            term = dot_t(reply_hi[0:n_dev, :], amp_parts[part])
            lit = term if part == 0 else lit + term
        reply_out[0] = lit
        near = dot_t(reply_hi[n_dev:, :], amp_parts[1]) + dot_t(reply_lo[...], amp_parts[0])
        near = near + dot_t(reply_hi[n_dev:, :], amp_parts[0])
        for r in range(3):
            reply_out[1 + r] = near[r * n_dev : (r + 1) * n_dev]

        def send(t):
            pltpu.make_async_remote_copy(
                reply_out.at[:, pl.ds(t, 1)],
                reply_in.at[:, pl.ds(me, 1)],
                reply_send,
                reply_recv,
                device_id=(t, core),
                device_id_type=MESH,
            ).start()

        each_peer(send)
        reply_in[:, pl.ds(me, 1), :] = reply_out[:, pl.ds(me, 1), :]

    def wait_reply(ref, sem):
        part = ref.at[:, pl.ds(0, n_dev - 1)]
        pltpu.make_async_copy(part, part, sem).wait()

    def wait_rows(ref, sem):
        part = ref.at[pl.ds(0, n_dev - 1)]
        pltpu.make_async_copy(part, part, sem).wait()

    theta_now[...] = theta_ref[...]
    reply()
    shape = (CAP * n_dev, 5 * 128)
    rest_mask[...] = jnp.where(
        iota(shape, 0) // n_dev == (iota(shape, 1) % 128) // K, 1.0, 0.0
    ).astype(BF16)
    own_obj = meta_in[1]
    turned = dot_t(
        jnp.where(iota((128, 128), 0) == iota((128, 128), 1), 1.0, 0.0).astype(BF16), own_obj.astype(BF16)
    )
    placed = dot(
        turned.astype(BF16),
        jnp.where(iota((n_dev, n_slot), 1) // CAP == iota((n_dev, n_slot), 0), 1.0, 0.0).astype(BF16),
    )[:CAP]
    mine = iota((CAP, n_slot), 1) % CAP == iota((CAP, n_slot), 0)
    obj_of_slot = jnp.sum(jnp.where(mine, placed, 0.0), axis=0, keepdims=True)
    member[...] = jnp.where(
        iota((n_obj, n_slot), 0).astype(F32) + 1.0 == obj_of_slot, 1.0, 0.0
    ).astype(BF16)
    obj_sub = iota((n_obj, n_dev), 0).astype(F32) + 1.0
    member2[...] = jnp.concatenate(
        [jnp.where(obj_sub == turned[c : c + 1], 1.0, 0.0) for c in range(CAP)], axis=1
    ).astype(BF16)
    for copy in in_copies[8:]:
        copy.wait()
    lax.fori_loop(0, n_chunk, build, 0)
    pltpu.make_async_copy(meta_part, meta_part, meta_send).wait()
    for copy in pixel_copies:
        copy.wait()

    fold_shape = (2 * CAP * K, 2 * K)
    fold_row, fold_col = iota(fold_shape, 0), iota(fold_shape, 1)
    fold = jnp.where(
        (fold_row // (CAP * K) == fold_col // K) & (fold_row % K == fold_col % K), 1.0, 0.0
    ).astype(BF16)

    def sweep(it, carry):
        wait_reply(reply_in, reply_recv)
        near = jnp.concatenate([reply_in[r] for r in (1, 2, 3)], axis=0)
        lit = dot_exact(from_lit[...], reply_in[0])
        near = dot_close(from_near[...], near)
        wide = jnp.concatenate([lit * gain_mask[...], near * plain_mask[...]], axis=1)
        coeff = dot(wide.astype(BF16), fold).astype(BF16)
        gain = stamp_cols[:, 0:1]
        softening = stamp_cols[:, 1:2]
        gram[...] = jnp.zeros_like(gram)
        proj[...] = jnp.zeros_like(proj)

        def one_chunk(i):
            resid = pixels[i].astype(F32) - dot(coeff, both[i])
            weight = ROBUST / (resid * resid + softening)
            gram[...] += dot_t(weight.astype(BF16), pair[i])
            proj[...] += dot_t(both[i, 0:K, :], (weight * resid).astype(BF16))

        for i in range(n_chunk):
            one_chunk(i)
        main = dot_close(to_slot[...], gram[:, :128] * (gain * gain))
        rest_proj = dot_t_exact(to_dest[...], jnp.concatenate([proj[...]] * CAP, axis=0) * gain_rows[...])
        rest_diag = dot_close(to_dest[...], gram[:, 128:] * (gain_mask[...] * gain))

        @pl.when(it > 0)
        def _():
            wait_rows(rows_out, rows_send)

        rows_out[:, 0:CAP, :] = main.reshape(n_dev, CAP, 128)
        rows_out[:, CAP, :] = rest_proj
        rows_out[:, CAP + 1, :] = rest_diag

        def send(t):
            pltpu.make_async_remote_copy(
                rows_out.at[t],
                rows_in.at[me],
                rows_send,
                rows_recv,
                device_id=(t, core),
                device_id_type=MESH,
            ).start()

        each_peer(send)
        rows_in[me] = rows_out[me]

        wait_rows(rows_in, rows_recv)
        main_sum = dot_close(member[...], rows_in[:, 0:CAP, :].reshape(n_slot, 128))
        parts = split3(rows_in[:, CAP, :]) + split(rows_in[:, CAP + 1, :])
        parts = jnp.concatenate(parts, axis=1)
        parts = dot(member2[...], jnp.concatenate([parts] * CAP, axis=0) * rest_mask[...])
        proj_sum = parts[:, 0:128] + (parts[:, 128:256] + parts[:, 256:384])
        rest_sum = jnp.concatenate([proj_sum, parts[:, 384:512] + parts[:, 512:640]], axis=1)
        sums = jnp.concatenate([main_sum, rest_sum], axis=1)
        sums_out[it] = sums
        copy = pltpu.make_async_remote_copy(
            sums_out.at[it],
            sums_in.at[it],
            sums_send.at[it],
            sums_recv.at[it],
            device_id=(me, 1 - core),
            device_id_type=MESH,
        )
        copy.start()
        copy.wait()
        full = dot_t_exact(table_ref[...], sums + sums_in[it])
        theta = theta_now[...]
        step = solve(full, jnp.exp(theta), theta, theta_ref[...])
        out_ref[0:K] = theta
        out_ref[K:] = step
        theta = theta + step
        theta_now[...] = theta
        wait_reply(reply_out, reply_send)

        @pl.when(it < ITERS - 1)
        def _():
            spread_amp(theta)
            reply()

        return carry

    lax.fori_loop(0, ITERS, sweep, 0)
    wait_rows(rows_out, rows_send)


def local(
    stamps,
    stamp_gain,
    stamp_invvar,
    stamp_dest,
    stamp_obj,
    phi_tpl,
    psi_tpl,
    theta_init,
    nb_id,
    nb_weight,
):
    n_dev = lax.axis_size("sky")
    n_stamp, n_band, pix = stamps.shape
    n_obj = theta_init.shape[1]
    chunk = pix
    n_chunk = n_band * (pix // chunk)
    table = jnp.asarray(expand_table(), BF16)
    n_slot = n_dev * CAP
    operands = (
        jnp.transpose(stamps, (1, 0, 2)),
        stamp_gain,
        stamp_invvar,
        stamp_dest.reshape(1, n_stamp),
        stamp_obj.reshape(1, n_stamp),
        phi_tpl,
        psi_tpl,
        theta_init,
        nb_id.T,
        nb_weight.T,
        table,
    )
    scratch = [pltpu.VMEM(a.shape, a.dtype) for a in operands[1:]] + [
        pltpu.VMEM((8, 128), F32),
        pltpu.VMEM((n_chunk, n_stamp, chunk), BF16),
        pltpu.VMEM((n_chunk, 256, chunk), BF16),
        pltpu.VMEM((n_chunk, 32, chunk), BF16),
        pltpu.VMEM((n_stamp, 256), F32),
        pltpu.VMEM((K, n_stamp), F32),
        pltpu.VMEM((n_slot, n_stamp), BF16),
        pltpu.VMEM((n_dev, n_stamp), BF16),
        pltpu.VMEM((n_stamp, n_dev), BF16),
        pltpu.VMEM((n_stamp, 3 * n_dev), BF16),
        pltpu.VMEM((n_stamp, 128), F32),
        pltpu.VMEM((128, n_stamp), F32),
        pltpu.VMEM((n_stamp, 128), F32),
        pltpu.VMEM((n_stamp, 128), F32),
        pltpu.VMEM((n_obj, n_slot), BF16),
        pltpu.VMEM((n_obj, n_slot), BF16),
        pltpu.VMEM((4 * n_dev, CAP * n_obj), BF16),
        pltpu.VMEM((3 * n_dev, CAP * n_obj), BF16),
        pltpu.VMEM((CAP * K, CAP * n_obj), BF16),
        pltpu.VMEM((CAP * n_dev, 5 * 128), BF16),
        pltpu.VMEM((3, CAP * K, CAP * n_obj), BF16),
        pltpu.VMEM((K, n_obj), F32),
        pltpu.VMEM((n_dev + 8, 128), F32),
        pltpu.VMEM((3, n_dev, 128), F32),
        pltpu.VMEM((2, 8, 128), F32),
        pltpu.VMEM((n_dev, CAP + 2, 128), F32),
        pltpu.VMEM((n_dev, CAP + 2, 128), F32),
        pltpu.VMEM((4, n_dev, 128), F32),
        pltpu.VMEM((4, n_dev, 128), F32),
        pltpu.VMEM((ITERS, n_obj, 384), F32),
        pltpu.VMEM((ITERS, n_obj, 384), F32),
        pltpu.SemaphoreType.DMA((10,)),
        pltpu.SemaphoreType.DMA((n_chunk,)),
        pltpu.SemaphoreType.DMA,
        pltpu.SemaphoreType.DMA,
        pltpu.SemaphoreType.DMA((2,)),
        pltpu.SemaphoreType.DMA((2,)),
        pltpu.SemaphoreType.DMA,
        pltpu.SemaphoreType.DMA,
        pltpu.SemaphoreType.DMA,
        pltpu.SemaphoreType.DMA,
        pltpu.SemaphoreType.DMA((ITERS,)),
        pltpu.SemaphoreType.DMA((ITERS,)),
    ]
    fitted = pl.pallas_call(
        functools.partial(kernel, (n_dev, n_stamp, n_obj, pix, chunk)),
        out_shape=jax.ShapeDtypeStruct((2 * K, n_obj), F32),
        in_specs=[pl.BlockSpec(memory_space=pltpu.HBM)] * len(operands),
        out_specs=pl.BlockSpec(memory_space=pltpu.VMEM),
        scratch_shapes=scratch,
        compiler_params=pltpu.CompilerParams(
            collective_id=0, has_side_effects=True, vmem_limit_bytes=(64 << 20) - (1 << 16)
        ),
    )(*operands)
    return fitted[:K] + fitted[K:]


def solution(mesh):
    in_specs = (
        P("sky", "band", None),
        P("sky"),
        P("sky"),
        P("sky", None),
        P("sky"),
        P("band", None, None),
        P("band", None, None),
        P(None, "sky"),
        P("sky", None),
        P("sky", None),
    )
    out_specs = P(None, "sky")
    return jax.shard_map(local, mesh=mesh, in_specs=in_specs, out_specs=out_specs, check_vma=False)
```
